32 devices in a mesh: row: 16 (over z, y, x), col: 2 (over core).
Axes of the slice: x: 2, y: 2, z: 4, core: 2. Of those that a mesh axis runs over, the one named last changes fastest.
Arguments:
- green_function: float32 [32, 32, 64, 128], P('row', 'col'), may hold values from -3 to 3
- hamiltonian: float32 [64, 128], replicated, may hold values from -3 to 3
Outputs:
- green_out: float32 [32, 32, 64, 128], P('row', 'col')
The draws below stay inside these ranges and needn't reach their ends.
All inputs are finite; a program needn't handle non-finite values.
Results may differ from the reference program's by a relative error of at most 0.00019.
Values sent between devices are 32-bit elements; how exact they have to be, the bound alone decides.
A program may use at most 64 MiB of HBM per device.

```python
import jax
import jax.numpy as jnp
from jax import lax

NORB = 64
STEPS = 2
NT = 32


def level_of(rng, shape, pieces, smallest, high):
    gain, own = 1.0, jax.random.fold_in(rng, 6)
    for position, parts in pieces:
        heights = jnp.exp(jax.random.uniform(jax.random.fold_in(own, position), (parts,), jnp.float32, smallest / len(pieces), high / len(pieces)))
        gain = gain * jnp.repeat(heights, shape[position] // parts).reshape([-1 if axis == position else 1 for axis in range(len(shape))])
    return gain


def noise(stream_key, shape, scale, most, shards=(), held_as=jnp.bfloat16):
    factor_of = level_of(stream_key, shape, shards, -0.22, 0.18) if shards else 1.0
    values = jax.random.normal(stream_key, shape, jnp.float32) * scale * factor_of
    return jnp.minimum(jnp.maximum(values, -most), most).astype(held_as)


def setup_inputs(seed: int = 0) -> dict:
    streams_of = jax.random.split(jax.random.key(seed), 3)
    return {
        "green_function": noise(streams_of[0], (NT, NT, NORB, 2 * NORB), 0.5, 3.0, ((0, 16), (1, 2)), jnp.float32),
        "hamiltonian": noise(streams_of[1], (NORB, 2 * NORB), 0.5, 3.0, (), jnp.float32),
    }


time_step = 0.1


def rotate(values):
    half = values.shape[-1] // 2
    return jnp.concatenate([-values[..., half:], values[..., :half]], axis=-1)


def advance(green_function, hamiltonian, weight):
    orbits = green_function.shape[2]
    count = green_function.shape[0]
    real_part = green_function[..., :orbits]
    imag_part = green_function[..., orbits:]
    magnitude = real_part * real_part + imag_part * imag_part
    scaled = jnp.concatenate([magnitude, magnitude], axis=-1) * green_function
    sigma = -(time_step * weight)[:, :, None, None] * scaled
    sigma_pair = jnp.concatenate([-sigma, rotate(sigma)], axis=2)

    def one_row(sigma_row):
        return jnp.einsum("sxq,uskq->ukx", sigma_row, green_function, precision=lax.Precision.HIGHEST)

    partial_value = lax.map(one_row, sigma_pair)
    integral = partial_value.reshape(count, count, orbits, 2, orbits).transpose(0, 1, 4, 3, 2).reshape(count, count, orbits, 2 * orbits)
    ham_real = hamiltonian[:, :orbits]
    ham_imag = hamiltonian[:, orbits:]
    driven = jnp.einsum("ij,tujq->tuiq", ham_real, green_function, precision=lax.Precision.HIGHEST)
    driven = driven + jnp.einsum("ij,tujq->tuiq", ham_imag, rotate(green_function), precision=lax.Precision.HIGHEST)
    driven = driven + integral
    return green_function - time_step * rotate(driven)


def reference(green_function, hamiltonian):
    count = green_function.shape[0]
    times = jnp.arange(count, dtype=jnp.int32)
    first = times[:, None]
    second = times[None, :]
    weight = jnp.where(second < first, jnp.float32(1.0), jnp.where(second == first, jnp.float32(0.5), jnp.float32(0.0)))
    weight = weight.astype(green_function.dtype)
    for repeat in range(STEPS):
        green_function = advance(green_function, hamiltonian, weight)
    return green_function
```

```python
import functools

import jax
import jax.numpy as jnp
from jax import lax
from jax.experimental import pallas as pl
from jax.experimental.pallas import tpu as pltpu
from jax.sharding import PartitionSpec as P

STEPS = 2
time_step = 0.1

GROUP = 4
CHUNK = 4
MESH = pl.DeviceIdType.MESH
NT = (((1,), (1,)), ((), ()))
NN = (((1,), (0,)), ((), ()))


def dot(a, b, dims):
    return lax.dot_general(a, b, dims, preferred_element_type=jnp.float32)


def split(x):
    hi = x.astype(jnp.bfloat16)
    lo = (x - hi.astype(jnp.float32)).astype(jnp.bfloat16)
    return hi, lo


def kernel(
    planes, cols, green, ham, out, held, plane, res, red_t, red_u,
    acc_t, acc_u, hat_hi, hat_lo, sig_hi, sig_lo, sx, hx_hi, hx_lo, h_acc,
    z_send, z_recv, x_send, y_send, f_send, p_recv,
    rt_send, rt_recv, ru_send, ru_recv, t_send, t_recv, u_send, u_recv,
):
    lr, lc, orb, wide = green.shape
    half = wide // 2
    B, A, C = GROUP, planes, cols
    pu = B * lr
    ppc = lc // pu
    ch = min(CHUNK, lc)
    nj = lc // ch
    kw = ch * wide

    row = lax.axis_index("row")
    col = lax.axis_index("col")
    z, p = row // B, row % B
    xn = p + 1 - 2 * (p % 2)
    yn = (p + 2) % B
    dn = (xn + 2) % B
    s_first = col * lc
    cz = z // ppc

    def dev(zz, pp, cc):
        return (zz * B + pp, cc)

    def remote(src, dst, ss, rs, to):
        return pltpu.make_async_remote_copy(
            src_ref=src, dst_ref=dst, send_sem=ss, recv_sem=rs, device_id=to, device_id_type=MESH
        )

    bar = pltpu.get_barrier_semaphore()
    for q in (xn, yn, dn):
        pl.semaphore_signal(bar, inc=1, device_id=dev(z, q, col), device_id_type=MESH)
    for k in range(1, A):
        pl.semaphore_signal(bar, inc=1, device_id=dev((z + k) % A, p, col), device_id_type=MESH)
    for k in range(1, C):
        pl.semaphore_signal(bar, inc=1, device_id=dev(z, p, (col + k) % C), device_id_type=MESH)

    lane = lax.broadcasted_iota(jnp.int32, (orb, wide), 1)
    sign = jnp.where(lane < half, jnp.float32(-1.0), jnp.float32(1.0))

    def rot(x):
        return pltpu.roll(x, half, 1) * sign

    def copy_in(i, _):
        h, m = i // lc, i % lc
        held[0, z, h, m] = green[h, m]
        return 0

    lax.fori_loop(0, lr * lc, copy_in, 0)
    pl.semaphore_wait(bar, (B - 1) + (A - 1) + (C - 1))

    ham_hi, ham_lo = split(ham[...])

    def needed(v, j):
        return s_first + j * ch <= (v * B + p) * lr + lr - 1

    def reached(j):
        return s_first + j * ch <= z * pu + pu - 1

    def hats(src, hi_ref, lo_ref, first):
        def one(i, _):
            h, m = i // lc, i % lc
            g = src[h, m]
            r0 = pl.multiple_of((first + h) * 2 * orb, 2 * orb)
            c0 = pl.multiple_of(m * wide, wide)
            hi, lo = split(g)
            hi_ref[pl.ds(r0, orb), pl.ds(c0, wide)] = hi
            lo_ref[pl.ds(r0, orb), pl.ds(c0, wide)] = lo
            hi, lo = split(rot(g))
            r1 = pl.multiple_of(r0 + orb, orb)
            hi_ref[pl.ds(r1, orb), pl.ds(c0, wide)] = hi
            lo_ref[pl.ds(r1, orb), pl.ds(c0, wide)] = lo
            return 0

        lax.fori_loop(0, lr * lc, one, 0)

    def sigma(g, t, m):
        s = s_first + m
        weight = jnp.where(s < t, jnp.float32(time_step), jnp.where(s == t, jnp.float32(0.5 * time_step), jnp.float32(0.0)))
        sq = g * g
        return split(weight * ((sq + pltpu.roll(sq, half, 1)) * g))

    def sigma_plane(src, q):
        def chunk(j, _):
            @pl.when(reached(j))
            def _():
                def one(i, _):
                    h, m = i // ch, j * ch + i % ch
                    hi, lo = sigma(src[h, m], (z * B + q) * lr + h, m)
                    r0 = pl.multiple_of((q * lr + h) * orb, orb)
                    c0 = pl.multiple_of(m * wide, wide)
                    sig_hi[pl.ds(r0, orb), pl.ds(c0, wide)] = hi
                    sig_lo[pl.ds(r0, orb), pl.ds(c0, wide)] = lo
                    return 0

                lax.fori_loop(0, lr * ch, one, 0)
            return 0

        lax.fori_loop(0, nj, chunk, 0)

    def step_body(step, _):
        own = held.at[step, z]

        def z_copy(v, j):
            part = held.at[step, v, :, pl.ds(j * ch, ch)]
            return remote(part, part, z_send.at[step, v, j], z_recv.at[step, v, j], dev((z + A - 1) % A, p, col))

        def each_chunk(v, action):
            def one(j, _):
                @pl.when(needed(v, j))
                def _():
                    action(v, j)
                return 0

            lax.fori_loop(0, nj, one, 0)

        def to_x(h):
            return remote(own.at[h], plane.at[step, p, h], x_send.at[step, h], p_recv.at[step, p, h], dev(z, xn, col))

        def to_y(h):
            return remote(own.at[h], plane.at[step, p, h], y_send.at[step, h], p_recv.at[step, p, h], dev(z, yn, col))

        def onward(h):
            src, to = (xn, yn) if h % 2 == 0 else (yn, xn)
            part = plane.at[step, src, h]
            return remote(part, part, f_send.at[step, h], p_recv.at[step, src, h], dev(z, to, col))

        def arrived(q, h):
            part = plane.at[step, q, h]
            remote(part, part, f_send.at[step, h], p_recv.at[step, q, h], dev(z, xn, col)).wait_recv()

        @pl.when(z > 0)
        def _():
            each_chunk(z, lambda v, j: z_copy(v, j).start())

        for h in range(lr):
            to_x(h).start()
            to_y(h).start()

        hats(own, hat_hi, hat_lo, p * lr)
        sigma_plane(own, p)
        for h in range(lr):
            r0 = pl.multiple_of((p * lr + h) * 2 * orb, 2 * orb)
            g_hi = hat_hi[pl.ds(r0, 2 * orb), :]
            g_lo = hat_lo[pl.ds(r0, 2 * orb), :]
            h_acc[pl.ds(h * orb, orb), :] = dot(ham_hi, g_hi, NN) + (dot(ham_hi, g_lo, NN) + dot(ham_lo, g_hi, NN))

        for h in range(lr):
            arrived(xn if h % 2 == 0 else yn, h)
            onward(h).start()

        def relay(v, j):
            z_copy(v, j).wait_recv()

            @pl.when(z > 0)
            def _():
                z_copy(v, j).start()

        @pl.when(z > 0)
        def _():
            @pl.when(z + 1 < A)
            def _():
                each_chunk(z + 1, relay)

        for h in range(lr):
            arrived(yn if h % 2 == 0 else xn, h)
        for q in (xn, yn):
            hats(plane.at[step, q], hat_hi, hat_lo, q * lr)
            sigma_plane(plane.at[step, q], q)

        @pl.when(z > 0)
        def _():
            def more(v, _):
                each_chunk(v, relay)
                return 0

            lax.fori_loop(z + 2, A, more, 0)

        for h in range(lr):
            arrived(dn, h)
        hats(plane.at[step, dn], hat_hi, hat_lo, dn * lr)
        sigma_plane(plane.at[step, dn], dn)

        def t_red(v, to):
            return remote(acc_t.at[v], red_t.at[step, v], rt_send.at[v], rt_recv.at[step, v], dev(z, p, to))

        def u_red(v, to):
            return remote(acc_u.at[v], red_u.at[step, v], ru_send.at[v], ru_recv.at[step, v], dev(z, p, to))

        def t_res(v):
            return remote(acc_t.at[v], res.at[step, z], t_send.at[v], t_recv.at[step, z], dev(v, p, col))

        def u_part(v, q, at):
            return (
                acc_u.at[v, pl.ds(pl.multiple_of(q * lr * orb, lr * orb), lr * orb), :],
                res.at[step, v, :, pl.ds(pl.multiple_of(at * lr * wide, lr * wide), lr * wide)],
            )

        def u_res(v, q):
            src, dst = u_part(v, q, p)
            return remote(src, dst, u_send.at[v, q], u_recv.at[step, v, p], dev(z, q, col))

        def place(owner):
            return (col + C - owner) % C

        down = (col + C - 1) % C

        def rows_v(v, _):
            @pl.when(v > z)
            def _():
                @pl.when(z == 0)
                def _():
                    each_chunk(v, lambda v, j: z_copy(v, j).wait_recv())

            acc_t[v] = jnp.zeros(acc_t.shape[1:], jnp.float32)

            def t_chunk(j, _):
                @pl.when(needed(v, j))
                def _():
                    def one(i, _):
                        h, m = i // ch, j * ch + i % ch
                        hi, lo = sigma(held[step, v, h, m], (v * B + p) * lr + h, m)
                        r0 = pl.multiple_of(h * orb, orb)
                        c0 = pl.multiple_of(m * wide, wide)
                        sx[pl.ds(r0, orb), pl.ds(c0, wide)] = hi
                        sx[pl.ds(pl.multiple_of(lr * orb + r0, orb), orb), pl.ds(c0, wide)] = lo
                        return 0

                    lax.fori_loop(0, lr * ch, one, 0)
                    ks = pl.ds(pl.multiple_of(j * kw, kw), kw)
                    both = dot(sx[:, ks], hat_hi[:, ks], NT)
                    low = dot(sx[pl.ds(0, lr * orb), ks], hat_lo[:, ks], NT)
                    acc_t[v] += both[: lr * orb] + (both[lr * orb :] + low)
                return 0

            lax.fori_loop(0, nj, t_chunk, 0)
            k = place(cz)
            if C > 1:
                @pl.when(k < C - 1)
                def _():
                    t_red(v, down).wait_recv()
                    acc_t[v] += red_t[step, v]

                @pl.when(k > 0)
                def _():
                    t_red(v, down).start()

            @pl.when(k == 0)
            def _():
                @pl.when(v > z)
                def _():
                    t_res(v).start()

                @pl.when(v == z)
                def _():
                    res[step, z] = acc_t[z]

            @pl.when(v > z)
            def _():
                hats(held.at[step, v], hx_hi, hx_lo, 0)
                acc_u[v] = jnp.zeros(acc_u.shape[1:], jnp.float32)

                def u_chunk(j, _):
                    @pl.when(reached(j))
                    def _():
                        ks = pl.ds(pl.multiple_of(j * kw, kw), kw)
                        hi, lo = sig_hi[:, ks], sig_lo[:, ks]
                        ghi, glo = hx_hi[:, ks], hx_lo[:, ks]
                        acc_u[v] += dot(hi, ghi, NT) + (dot(hi, glo, NT) + dot(lo, ghi, NT))
                    return 0

                lax.fori_loop(0, nj, u_chunk, 0)
                k = place(v // ppc)
                if C > 1:
                    @pl.when(k < C - 1)
                    def _():
                        u_red(v, down).wait_recv()
                        acc_u[v] += red_u[step, v]

                    @pl.when(k > 0)
                    def _():
                        u_red(v, down).start()

                @pl.when(k == 0)
                def _():
                    for q in (xn, yn, dn):
                        u_res(v, q).start()
                    src, dst = u_part(v, p, p)
                    dst[...] = src[...]
            return 0

        lax.fori_loop(z, A, rows_v, 0)

        def collect(i, _):
            w = col * ppc + i

            @pl.when(w < z)
            def _():
                part = res.at[step, w]
                remote(part, part, t_send.at[w], t_recv.at[step, w], dev(z, xn, col)).wait_recv()

            @pl.when(w > z)
            def _():
                for q in (xn, yn, dn):
                    part = res.at[step, w, :, pl.ds(pl.multiple_of(q * lr * wide, lr * wide), lr * wide)]
                    remote(part, part, u_send.at[w, q], u_recv.at[step, w, q], dev(z, xn, col)).wait_recv()

            def update(i, _):
                h, m = i // pu, i % pu
                u = (w - col * ppc) * pu + m
                r0 = pl.multiple_of(h * orb, orb)
                driven = h_acc[pl.ds(r0, orb), pl.ds(pl.multiple_of(u * wide, wide), wide)]
                driven = driven + res[step, w, pl.ds(r0, orb), pl.ds(pl.multiple_of(m * wide, wide), wide)]
                new = held[step, z, h, u] - time_step * rot(driven)

                @pl.when(step < STEPS - 1)
                def _():
                    held[step + 1, z, h, u] = new

                @pl.when(step == STEPS - 1)
                def _():
                    out[h, u] = new
                return 0

            lax.fori_loop(0, lr * pu, update, 0)
            return 0

        lax.fori_loop(0, ppc, collect, 0)

        for h in range(lr):
            to_x(h).wait_send()
            to_y(h).wait_send()
            onward(h).wait_send()

        def sent(v, _):
            @pl.when(z > 0)
            def _():
                each_chunk(v, lambda v, j: z_copy(v, j).wait_send())

            k = place(cz)

            @pl.when(k > 0)
            def _():
                t_red(v, down).wait_send()

            @pl.when(v > z)
            def _():
                @pl.when(k == 0)
                def _():
                    t_res(v).wait_send()

                ku = place(v // ppc)

                @pl.when(ku > 0)
                def _():
                    u_red(v, down).wait_send()

                @pl.when(ku == 0)
                def _():
                    for q in (xn, yn, dn):
                        u_res(v, q).wait_send()
            return 0

        lax.fori_loop(z, A, sent, 0)
        return 0

    lax.fori_loop(0, STEPS, step_body, 0)


def solution(mesh):
    rows, cols = mesh.shape["row"], mesh.shape["col"]
    planes = rows // GROUP

    def step(green, ham):
        lr, lc, orb, wide = green.shape
        pu = GROUP * lr
        nj = lc // min(CHUNK, lc)
        f32, bf16 = jnp.float32, jnp.bfloat16
        dma = pltpu.SemaphoreType.DMA
        big = (lr * orb, pu * wide)
        tall = (pu * orb, lr * wide)
        return pl.pallas_call(
            functools.partial(kernel, planes, cols),
            out_shape=jax.ShapeDtypeStruct(green.shape, f32),
            in_specs=[pl.BlockSpec(memory_space=pltpu.VMEM)] * 2,
            out_specs=pl.BlockSpec(memory_space=pltpu.VMEM),
            scratch_shapes=[
                pltpu.VMEM((STEPS, planes) + green.shape, f32),
                pltpu.VMEM((STEPS, GROUP) + green.shape, f32),
                pltpu.VMEM((STEPS, planes) + big, f32),
                pltpu.VMEM((STEPS, planes) + big, f32),
                pltpu.VMEM((STEPS, planes) + tall, f32),
                pltpu.VMEM((planes,) + big, f32),
                pltpu.VMEM((planes,) + tall, f32),
                pltpu.VMEM((pu * wide, lc * wide), bf16),
                pltpu.VMEM((pu * wide, lc * wide), bf16),
                pltpu.VMEM((pu * orb, lc * wide), bf16),
                pltpu.VMEM((pu * orb, lc * wide), bf16),
                pltpu.VMEM((2 * lr * orb, lc * wide), bf16),
                pltpu.VMEM((lr * wide, lc * wide), bf16),
                pltpu.VMEM((lr * wide, lc * wide), bf16),
                pltpu.VMEM((lr * orb, lc * wide), f32),
                dma((STEPS, planes, nj)), dma((STEPS, planes, nj)),
                dma((STEPS, lr)), dma((STEPS, lr)), dma((STEPS, lr)),
                dma((STEPS, GROUP, lr)),
                dma((planes,)), dma((STEPS, planes)),
                dma((planes,)), dma((STEPS, planes)),
                dma((planes,)), dma((STEPS, planes)),
                dma((planes, GROUP)), dma((STEPS, planes, GROUP)),
            ],
            compiler_params=pltpu.CompilerParams(
                collective_id=0, has_side_effects=True, vmem_limit_bytes=62 * 1024 * 1024
            ),
        )(green, ham)

    spec = P("row", "col", None, None)
    return jax.shard_map(step, mesh=mesh, in_specs=(spec, P()), out_specs=spec, check_vma=False)
```

```python
import functools

import jax
import jax.numpy as jnp
from jax import lax
from jax.experimental import pallas as pl
from jax.experimental.pallas import tpu as pltpu
from jax.sharding import PartitionSpec as P

STEPS = 2
time_step = 0.1

GROUP = 4
UNROLL = 8
CHUNK = 4
MESH = pl.DeviceIdType.MESH
NT = (((1,), (1,)), ((), ()))
NN = (((1,), (0,)), ((), ()))


def dot(a, b, dims):
    return lax.dot_general(a, b, dims, preferred_element_type=jnp.float32)


def split(x):
    hi = x.astype(jnp.bfloat16)
    lo = (x - hi.astype(jnp.float32)).astype(jnp.bfloat16)
    return hi, lo


def kernel(
    planes, cols, green, ham, out, held, plane, res, red_t, red_u,
    acc_t, acc_u, hat_hi, hat_lo, sig_hi, sig_lo, sx, hx_hi, hx_lo, h_acc,
    z_send, z_recv, x_send, y_send, f_send, p_recv,
    rt_send, rt_recv, ru_send, ru_recv, t_send, t_recv, u_send, u_recv,
):
    lr, lc, orb, wide = green.shape
    half = wide // 2
    B, A, C = GROUP, planes, cols
    pu = B * lr
    ppc = lc // pu
    ch = min(CHUNK, lc)
    nj = lc // ch
    kw = ch * wide

    row = lax.axis_index("row")
    col = lax.axis_index("col")
    z, p = row // B, row % B
    xn = p + 1 - 2 * (p % 2)
    yn = (p + 2) % B
    dn = (xn + 2) % B
    s_first = col * lc
    cz = z // ppc

    def dev(zz, pp, cc):
        return (zz * B + pp, cc)

    def remote(src, dst, ss, rs, to):
        return pltpu.make_async_remote_copy(
            src_ref=src, dst_ref=dst, send_sem=ss, recv_sem=rs, device_id=to, device_id_type=MESH
        )

    bar = pltpu.get_barrier_semaphore()
    for q in (xn, yn, dn):
        pl.semaphore_signal(bar, inc=1, device_id=dev(z, q, col), device_id_type=MESH)
    for k in range(1, A):
        pl.semaphore_signal(bar, inc=1, device_id=dev((z + k) % A, p, col), device_id_type=MESH)
    for k in range(1, C):
        pl.semaphore_signal(bar, inc=1, device_id=dev(z, p, (col + k) % C), device_id_type=MESH)

    lane = lax.broadcasted_iota(jnp.int32, (orb, wide), 1)
    sign = jnp.where(lane < half, jnp.float32(-1.0), jnp.float32(1.0))

    def rot(x):
        return pltpu.roll(x, half, 1) * sign

    def copy_in(i, _):
        h, m = i // lc, i % lc
        held[0, z, h, m] = green[h, m]
        return 0

    lax.fori_loop(0, lr * lc, copy_in, 0, unroll=UNROLL)
    pl.semaphore_wait(bar, (B - 1) + (A - 1) + (C - 1))

    ham_hi, ham_lo = split(ham[...])

    def needed(v, j):
        return s_first + j * ch <= (v * B + p) * lr + lr - 1

    def reached(j):
        return s_first + j * ch <= z * pu + pu - 1

    def hats(src, hi_ref, lo_ref, first):
        def one(i, _):
            h, m = i // lc, i % lc
            g = src[h, m]
            r0 = pl.multiple_of((first + h) * 2 * orb, 2 * orb)
            c0 = pl.multiple_of(m * wide, wide)
            hi, lo = split(g)
            hi_ref[pl.ds(r0, orb), pl.ds(c0, wide)] = hi
            lo_ref[pl.ds(r0, orb), pl.ds(c0, wide)] = lo
            hi, lo = split(rot(g))
            r1 = pl.multiple_of(r0 + orb, orb)
            hi_ref[pl.ds(r1, orb), pl.ds(c0, wide)] = hi
            lo_ref[pl.ds(r1, orb), pl.ds(c0, wide)] = lo
            return 0

        lax.fori_loop(0, lr * lc, one, 0, unroll=UNROLL)

    def sigma(g, t, m):
        s = s_first + m
        weight = jnp.where(s < t, jnp.float32(time_step), jnp.where(s == t, jnp.float32(0.5 * time_step), jnp.float32(0.0)))
        sq = g * g
        return split(weight * ((sq + pltpu.roll(sq, half, 1)) * g))

    def sigma_plane(src, q):
        def chunk(j, _):
            @pl.when(reached(j))
            def _():
                def one(i, _):
                    h, m = i // ch, j * ch + i % ch
                    hi, lo = sigma(src[h, m], (z * B + q) * lr + h, m)
                    r0 = pl.multiple_of((q * lr + h) * orb, orb)
                    c0 = pl.multiple_of(m * wide, wide)
                    sig_hi[pl.ds(r0, orb), pl.ds(c0, wide)] = hi
                    sig_lo[pl.ds(r0, orb), pl.ds(c0, wide)] = lo
                    return 0

                lax.fori_loop(0, lr * ch, one, 0, unroll=UNROLL)
            return 0

        lax.fori_loop(0, nj, chunk, 0)

    def step_body(step, _):
        own = held.at[step, z]

        def z_copy(v, j):
            part = held.at[step, v, :, pl.ds(j * ch, ch)]
            return remote(part, part, z_send.at[step, v, j], z_recv.at[step, v, j], dev((z + A - 1) % A, p, col))

        def each_chunk(v, action):
            def one(j, _):
                @pl.when(needed(v, j))
                def _():
                    action(v, j)
                return 0

            lax.fori_loop(0, nj, one, 0)

        def to_x(h):
            return remote(own.at[h], plane.at[step, p, h], x_send.at[step, h], p_recv.at[step, p, h], dev(z, xn, col))

        def to_y(h):
            return remote(own.at[h], plane.at[step, p, h], y_send.at[step, h], p_recv.at[step, p, h], dev(z, yn, col))

        def onward(h):
            src, to = (xn, yn) if h % 2 == 0 else (yn, xn)
            part = plane.at[step, src, h]
            return remote(part, part, f_send.at[step, h], p_recv.at[step, src, h], dev(z, to, col))

        def arrived(q, h):
            part = plane.at[step, q, h]
            remote(part, part, f_send.at[step, h], p_recv.at[step, q, h], dev(z, xn, col)).wait_recv()

        @pl.when(z > 0)
        def _():
            each_chunk(z, lambda v, j: z_copy(v, j).start())

        for h in range(lr):
            to_x(h).start()
            to_y(h).start()

        hats(own, hat_hi, hat_lo, p * lr)
        sigma_plane(own, p)
        for h in range(lr):
            r0 = pl.multiple_of((p * lr + h) * 2 * orb, 2 * orb)
            g_hi = hat_hi[pl.ds(r0, 2 * orb), :]
            g_lo = hat_lo[pl.ds(r0, 2 * orb), :]
            h_acc[pl.ds(h * orb, orb), :] = dot(ham_hi, g_hi, NN) + (dot(ham_hi, g_lo, NN) + dot(ham_lo, g_hi, NN))

        for h in range(lr):
            arrived(xn if h % 2 == 0 else yn, h)
            onward(h).start()

        def relay(v, j):
            z_copy(v, j).wait_recv()

            @pl.when(z > 0)
            def _():
                z_copy(v, j).start()

        @pl.when(z > 0)
        def _():
            @pl.when(z + 1 < A)
            def _():
                each_chunk(z + 1, relay)

        for h in range(lr):
            arrived(yn if h % 2 == 0 else xn, h)
        for q in (xn, yn):
            hats(plane.at[step, q], hat_hi, hat_lo, q * lr)
            sigma_plane(plane.at[step, q], q)

        @pl.when(z > 0)
        def _():
            def more(v, _):
                each_chunk(v, relay)
                return 0

            lax.fori_loop(z + 2, A, more, 0)

        for h in range(lr):
            arrived(dn, h)
        hats(plane.at[step, dn], hat_hi, hat_lo, dn * lr)
        sigma_plane(plane.at[step, dn], dn)

        def t_red(v, to):
            return remote(acc_t.at[v], red_t.at[step, v], rt_send.at[v], rt_recv.at[step, v], dev(z, p, to))

        def u_red(v, to):
            return remote(acc_u.at[v], red_u.at[step, v], ru_send.at[v], ru_recv.at[step, v], dev(z, p, to))

        def t_res(v):
            return remote(acc_t.at[v], res.at[step, z], t_send.at[v], t_recv.at[step, z], dev(v, p, col))

        def u_part(v, q, at):
            return (
                acc_u.at[v, pl.ds(pl.multiple_of(q * lr * orb, lr * orb), lr * orb), :],
                res.at[step, v, :, pl.ds(pl.multiple_of(at * lr * wide, lr * wide), lr * wide)],
            )

        def u_res(v, q):
            src, dst = u_part(v, q, p)
            return remote(src, dst, u_send.at[v, q], u_recv.at[step, v, p], dev(z, q, col))

        def place(owner):
            return (col + C - owner) % C

        down = (col + C - 1) % C

        def rows_v(v, _):
            @pl.when(v > z)
            def _():
                @pl.when(z == 0)
                def _():
                    each_chunk(v, lambda v, j: z_copy(v, j).wait_recv())

            acc_t[v] = jnp.zeros(acc_t.shape[1:], jnp.float32)

            def t_chunk(j, _):
                @pl.when(needed(v, j))
                def _():
                    def one(i, _):
                        h, m = i // ch, j * ch + i % ch
                        hi, lo = sigma(held[step, v, h, m], (v * B + p) * lr + h, m)
                        r0 = pl.multiple_of(h * orb, orb)
                        c0 = pl.multiple_of(m * wide, wide)
                        sx[pl.ds(r0, orb), pl.ds(c0, wide)] = hi
                        sx[pl.ds(pl.multiple_of(lr * orb + r0, orb), orb), pl.ds(c0, wide)] = lo
                        return 0

                    lax.fori_loop(0, lr * ch, one, 0, unroll=UNROLL)
                    ks = pl.ds(pl.multiple_of(j * kw, kw), kw)
                    both = dot(sx[:, ks], hat_hi[:, ks], NT)
                    low = dot(sx[pl.ds(0, lr * orb), ks], hat_lo[:, ks], NT)
                    acc_t[v] += both[: lr * orb] + (both[lr * orb :] + low)
                return 0

            lax.fori_loop(0, nj, t_chunk, 0)
            k = place(cz)
            if C > 1:
                @pl.when(k < C - 1)
                def _():
                    t_red(v, down).wait_recv()
                    acc_t[v] += red_t[step, v]

                @pl.when(k > 0)
                def _():
                    t_red(v, down).start()

            @pl.when(k == 0)
            def _():
                @pl.when(v > z)
                def _():
                    t_res(v).start()

                @pl.when(v == z)
                def _():
                    res[step, z] = acc_t[z]

            @pl.when(v > z)
            def _():
                hats(held.at[step, v], hx_hi, hx_lo, 0)
                acc_u[v] = jnp.zeros(acc_u.shape[1:], jnp.float32)

                def u_chunk(j, _):
                    @pl.when(reached(j))
                    def _():
                        ks = pl.ds(pl.multiple_of(j * kw, kw), kw)
                        hi, lo = sig_hi[:, ks], sig_lo[:, ks]
                        ghi, glo = hx_hi[:, ks], hx_lo[:, ks]
                        acc_u[v] += dot(hi, ghi, NT) + (dot(hi, glo, NT) + dot(lo, ghi, NT))
                    return 0

                lax.fori_loop(0, nj, u_chunk, 0)
                k = place(v // ppc)
                if C > 1:
                    @pl.when(k < C - 1)
                    def _():
                        u_red(v, down).wait_recv()
                        acc_u[v] += red_u[step, v]

                    @pl.when(k > 0)
                    def _():
                        u_red(v, down).start()

                @pl.when(k == 0)
                def _():
                    for q in (xn, yn, dn):
                        u_res(v, q).start()
                    src, dst = u_part(v, p, p)
                    dst[...] = src[...]
            return 0

        lax.fori_loop(z, A, rows_v, 0)

        def collect(i, _):
            w = col * ppc + i

            @pl.when(w < z)
            def _():
                part = res.at[step, w]
                remote(part, part, t_send.at[w], t_recv.at[step, w], dev(z, xn, col)).wait_recv()

            @pl.when(w > z)
            def _():
                for q in (xn, yn, dn):
                    part = res.at[step, w, :, pl.ds(pl.multiple_of(q * lr * wide, lr * wide), lr * wide)]
                    remote(part, part, u_send.at[w, q], u_recv.at[step, w, q], dev(z, xn, col)).wait_recv()

            def update(i, _):
                h, m = i // pu, i % pu
                u = (w - col * ppc) * pu + m
                r0 = pl.multiple_of(h * orb, orb)
                driven = h_acc[pl.ds(r0, orb), pl.ds(pl.multiple_of(u * wide, wide), wide)]
                driven = driven + res[step, w, pl.ds(r0, orb), pl.ds(pl.multiple_of(m * wide, wide), wide)]
                new = held[step, z, h, u] - time_step * rot(driven)

                @pl.when(step < STEPS - 1)
                def _():
                    held[step + 1, z, h, u] = new

                @pl.when(step == STEPS - 1)
                def _():
                    out[h, u] = new
                return 0

            lax.fori_loop(0, lr * pu, update, 0, unroll=UNROLL)
            return 0

        lax.fori_loop(0, ppc, collect, 0)

        for h in range(lr):
            to_x(h).wait_send()
            to_y(h).wait_send()
            onward(h).wait_send()

        def sent(v, _):
            @pl.when(z > 0)
            def _():
                each_chunk(v, lambda v, j: z_copy(v, j).wait_send())

            k = place(cz)

            @pl.when(k > 0)
            def _():
                t_red(v, down).wait_send()

            @pl.when(v > z)
            def _():
                @pl.when(k == 0)
                def _():
                    t_res(v).wait_send()

                ku = place(v // ppc)

                @pl.when(ku > 0)
                def _():
                    u_red(v, down).wait_send()

                @pl.when(ku == 0)
                def _():
                    for q in (xn, yn, dn):
                        u_res(v, q).wait_send()
            return 0

        lax.fori_loop(z, A, sent, 0)
        return 0

    lax.fori_loop(0, STEPS, step_body, 0)


def solution(mesh):
    rows, cols = mesh.shape["row"], mesh.shape["col"]
    planes = rows // GROUP

    def step(green, ham):
        lr, lc, orb, wide = green.shape
        pu = GROUP * lr
        nj = lc // min(CHUNK, lc)
        f32, bf16 = jnp.float32, jnp.bfloat16
        dma = pltpu.SemaphoreType.DMA
        big = (lr * orb, pu * wide)
        tall = (pu * orb, lr * wide)
        return pl.pallas_call(
            functools.partial(kernel, planes, cols),
            out_shape=jax.ShapeDtypeStruct(green.shape, f32),
            in_specs=[pl.BlockSpec(memory_space=pltpu.VMEM)] * 2,
            out_specs=pl.BlockSpec(memory_space=pltpu.VMEM),
            scratch_shapes=[
                pltpu.VMEM((STEPS, planes) + green.shape, f32),
                pltpu.VMEM((STEPS, GROUP) + green.shape, f32),
                pltpu.VMEM((STEPS, planes) + big, f32),
                pltpu.VMEM((STEPS, planes) + big, f32),
                pltpu.VMEM((STEPS, planes) + tall, f32),
                pltpu.VMEM((planes,) + big, f32),
                pltpu.VMEM((planes,) + tall, f32),
                pltpu.VMEM((pu * wide, lc * wide), bf16),
                pltpu.VMEM((pu * wide, lc * wide), bf16),
                pltpu.VMEM((pu * orb, lc * wide), bf16),
                pltpu.VMEM((pu * orb, lc * wide), bf16),
                pltpu.VMEM((2 * lr * orb, lc * wide), bf16),
                pltpu.VMEM((lr * wide, lc * wide), bf16),
                pltpu.VMEM((lr * wide, lc * wide), bf16),
                pltpu.VMEM((lr * orb, lc * wide), f32),
                dma((STEPS, planes, nj)), dma((STEPS, planes, nj)),
                dma((STEPS, lr)), dma((STEPS, lr)), dma((STEPS, lr)),
                dma((STEPS, GROUP, lr)),
                dma((planes,)), dma((STEPS, planes)),
                dma((planes,)), dma((STEPS, planes)),
                dma((planes,)), dma((STEPS, planes)),
                dma((planes, GROUP)), dma((STEPS, planes, GROUP)),
            ],
            compiler_params=pltpu.CompilerParams(
                collective_id=0, has_side_effects=True, vmem_limit_bytes=62 * 1024 * 1024
            ),
        )(green, ham)

    spec = P("row", "col", None, None)
    return jax.shard_map(step, mesh=mesh, in_specs=(spec, P()), out_specs=spec, check_vma=False)
```

```python
import functools

import jax
import jax.numpy as jnp
from jax import lax
from jax.experimental import pallas as pl
from jax.experimental.pallas import tpu as pltpu
from jax.sharding import PartitionSpec as P

STEPS = 2
time_step = 0.1

GROUP = 4
UNROLL = 8
CHUNK = 4
MESH = pl.DeviceIdType.MESH
NT = (((1,), (1,)), ((), ()))
NN = (((1,), (0,)), ((), ()))


def dot(a, b, dims):
    return lax.dot_general(a, b, dims, preferred_element_type=jnp.float32)


def split(x):
    hi = x.astype(jnp.bfloat16)
    lo = (x - hi.astype(jnp.float32)).astype(jnp.bfloat16)
    return hi, lo


def kernel(
    planes, cols, green, ham, out, held, plane, res, red_t, red_u,
    acc_t, acc_u, hat_hi, hat_lo, sig_hi, sig_lo, sx, hx_hi, hx_lo, h_acc,
    z_send, z_recv, x_send, y_send, f_send, p_recv,
    rt_send, rt_recv, ru_send, ru_recv, t_send, t_recv, u_send, u_recv,
):
    lr, lc, orb, wide = green.shape
    half = wide // 2
    B, A, C = GROUP, planes, cols
    pu = B * lr
    ppc = lc // pu
    ch = min(CHUNK, lc)
    nj = lc // ch
    kw = ch * wide

    row = lax.axis_index("row")
    col = lax.axis_index("col")
    z, p = row // B, row % B
    xn = p + 1 - 2 * (p % 2)
    yn = (p + 2) % B
    dn = (xn + 2) % B
    s_first = col * lc
    cz = z // ppc

    def dev(zz, pp, cc):
        return (zz * B + pp, cc)

    def remote(src, dst, ss, rs, to):
        return pltpu.make_async_remote_copy(
            src_ref=src, dst_ref=dst, send_sem=ss, recv_sem=rs, device_id=to, device_id_type=MESH
        )

    bar = pltpu.get_barrier_semaphore()
    for q in (xn, yn, dn):
        pl.semaphore_signal(bar, inc=1, device_id=dev(z, q, col), device_id_type=MESH)
    for k in range(1, A):
        pl.semaphore_signal(bar, inc=1, device_id=dev((z + k) % A, p, col), device_id_type=MESH)
    for k in range(1, C):
        pl.semaphore_signal(bar, inc=1, device_id=dev(z, p, (col + k) % C), device_id_type=MESH)

    lane = lax.broadcasted_iota(jnp.int32, (orb, wide), 1)
    sign = jnp.where(lane < half, jnp.float32(-1.0), jnp.float32(1.0))

    def rot(x):
        return pltpu.roll(x, half, 1) * sign

    def copy_in(i, _):
        h, m = i // lc, i % lc
        held[0, z, h, m] = green[h, m]
        return 0

    lax.fori_loop(0, lr * lc, copy_in, 0, unroll=UNROLL)
    pl.semaphore_wait(bar, (B - 1) + (A - 1) + (C - 1))

    ham_hi, ham_lo = split(ham[...])

    def needed(v, j):
        return s_first + j * ch <= (v * B + p) * lr + lr - 1

    def reached(j):
        return s_first + j * ch <= z * pu + pu - 1

    def hats(src, hi_ref, lo_ref, first):
        def one(i, _):
            h, m = i // lc, i % lc
            g = src[h, m]
            r0 = pl.multiple_of((first + h) * 2 * orb, 2 * orb)
            c0 = pl.multiple_of(m * wide, wide)
            hi, lo = split(g)
            hi_ref[pl.ds(r0, orb), pl.ds(c0, wide)] = hi
            lo_ref[pl.ds(r0, orb), pl.ds(c0, wide)] = lo
            hi, lo = split(rot(g))
            r1 = pl.multiple_of(r0 + orb, orb)
            hi_ref[pl.ds(r1, orb), pl.ds(c0, wide)] = hi
            lo_ref[pl.ds(r1, orb), pl.ds(c0, wide)] = lo
            return 0

        lax.fori_loop(0, lr * lc, one, 0, unroll=UNROLL)

    def sigma(g, t, m):
        s = s_first + m
        weight = jnp.where(s < t, jnp.float32(time_step), jnp.where(s == t, jnp.float32(0.5 * time_step), jnp.float32(0.0)))
        sq = g * g
        return split(weight * ((sq + pltpu.roll(sq, half, 1)) * g))

    def sigma_plane(src, q):
        def chunk(j, _):
            @pl.when(reached(j))
            def _():
                def one(i, _):
                    h, m = i // ch, j * ch + i % ch
                    hi, lo = sigma(src[h, m], (z * B + q) * lr + h, m)
                    r0 = pl.multiple_of((q * lr + h) * orb, orb)
                    c0 = pl.multiple_of(m * wide, wide)
                    sig_hi[pl.ds(r0, orb), pl.ds(c0, wide)] = hi
                    sig_lo[pl.ds(r0, orb), pl.ds(c0, wide)] = lo
                    return 0

                lax.fori_loop(0, lr * ch, one, 0, unroll=UNROLL)
            return 0

        lax.fori_loop(0, nj, chunk, 0)

    def step_body(step, _):
        own = held.at[step, z]

        def z_copy(v, j):
            part = held.at[step, v, :, pl.ds(j * ch, ch)]
            return remote(part, part, z_send.at[step, v, j], z_recv.at[step, v, j], dev((z + A - 1) % A, p, col))

        def each_chunk(v, action):
            def one(j, _):
                @pl.when(needed(v, j))
                def _():
                    action(v, j)
                return 0

            lax.fori_loop(0, nj, one, 0)

        def to_x(h):
            return remote(own.at[h], plane.at[step, p, h], x_send.at[step, h], p_recv.at[step, p, h], dev(z, xn, col))

        def to_y(h):
            return remote(own.at[h], plane.at[step, p, h], y_send.at[step, h], p_recv.at[step, p, h], dev(z, yn, col))

        def onward(h):
            src, to = (xn, yn) if h % 2 == 0 else (yn, xn)
            part = plane.at[step, src, h]
            return remote(part, part, f_send.at[step, h], p_recv.at[step, src, h], dev(z, to, col))

        def arrived(q, h):
            part = plane.at[step, q, h]
            remote(part, part, f_send.at[step, h], p_recv.at[step, q, h], dev(z, xn, col)).wait_recv()

        @pl.when(z > 0)
        def _():
            each_chunk(z, lambda v, j: z_copy(v, j).start())

        for h in range(lr):
            to_x(h).start()
            to_y(h).start()

        def cols_of(j):
            return pl.ds(pl.multiple_of(j * kw, kw), kw)

        def build(v, j):
            def one(i, _):
                h, m = i // ch, j * ch + i % ch
                hi, lo = sigma(held[step, v, h, m], (v * B + p) * lr + h, m)
                r0 = pl.multiple_of(h * orb, orb)
                c0 = pl.multiple_of(m * wide, wide)
                sx[v, pl.ds(r0, orb), pl.ds(c0, wide)] = hi
                sx[v, pl.ds(pl.multiple_of(lr * orb + r0, orb), orb), pl.ds(c0, wide)] = lo
                return 0

            lax.fori_loop(0, lr * ch, one, 0, unroll=UNROLL)

        def t_dot(v, j, q=None):
            ks = cols_of(j)
            us = pl.ds(0, pu * wide) if q is None else pl.ds(pl.multiple_of(q * lr * wide, lr * wide), lr * wide)
            both = dot(sx[v, :, ks], hat_hi[us, ks], NT)
            low = dot(sx[v, pl.ds(0, lr * orb), ks], hat_lo[us, ks], NT)
            acc_t[v, :, us] += both[: lr * orb] + (both[lr * orb :] + low)

        def t_rows(v, *qs):
            def one(v, j):
                for q in qs:
                    t_dot(v, j, q)

            each_chunk(v, one)

        def u_dot(v, j):
            @pl.when(reached(j))
            def _():
                def one(i, _):
                    h, m = i // ch, j * ch + i % ch
                    g = held[step, v, h, m]
                    r0 = pl.multiple_of(h * 2 * orb, 2 * orb)
                    r1 = pl.multiple_of(r0 + orb, orb)
                    c0 = pl.multiple_of((i % ch) * wide, wide)
                    hi, lo = split(g)
                    hx_hi[pl.ds(r0, orb), pl.ds(c0, wide)] = hi
                    hx_lo[pl.ds(r0, orb), pl.ds(c0, wide)] = lo
                    hi, lo = split(rot(g))
                    hx_hi[pl.ds(r1, orb), pl.ds(c0, wide)] = hi
                    hx_lo[pl.ds(r1, orb), pl.ds(c0, wide)] = lo
                    return 0

                lax.fori_loop(0, lr * ch, one, 0, unroll=UNROLL)
                ks = cols_of(j)
                hi, lo = sig_hi[:, ks], sig_lo[:, ks]
                ghi, glo = hx_hi[...], hx_lo[...]
                acc_u[v] += dot(hi, ghi, NT) + (dot(hi, glo, NT) + dot(lo, ghi, NT))

        def t_red(v, to):
            return remote(acc_t.at[v], red_t.at[step, v], rt_send.at[v], rt_recv.at[step, v], dev(z, p, to))

        def u_red(v, to):
            return remote(acc_u.at[v], red_u.at[step, v], ru_send.at[v], ru_recv.at[step, v], dev(z, p, to))

        def t_res(v):
            return remote(acc_t.at[v], res.at[step, z], t_send.at[v], t_recv.at[step, z], dev(v, p, col))

        def u_part(v, q, at):
            return (
                acc_u.at[v, pl.ds(pl.multiple_of(q * lr * orb, lr * orb), lr * orb), :],
                res.at[step, v, :, pl.ds(pl.multiple_of(at * lr * wide, lr * wide), lr * wide)],
            )

        def u_res(v, q):
            src, dst = u_part(v, q, p)
            return remote(src, dst, u_send.at[v, q], u_recv.at[step, v, p], dev(z, q, col))

        def place(owner):
            return (col + C - owner) % C

        down = (col + C - 1) % C

        def t_finish(v):
            k = place(cz)
            if C > 1:
                @pl.when(k > 0)
                def _():
                    if C > 2:
                        @pl.when(k < C - 1)
                        def _():
                            t_red(v, down).wait_recv()
                            acc_t[v] += red_t[step, v]

                    t_red(v, down).start()

            @pl.when(k == 0)
            def _():
                if C > 1:
                    t_red(v, down).wait_recv()

                @pl.when(v > z)
                def _():
                    if C > 1:
                        acc_t[v] += red_t[step, v]
                    t_res(v).start()

                @pl.when(v == z)
                def _():
                    if C > 1:
                        res[step, z] = acc_t[z] + red_t[step, z]
                    else:
                        res[step, z] = acc_t[z]

        def u_finish(v):
            k = place(v // ppc)
            if C > 1:
                @pl.when(k < C - 1)
                def _():
                    u_red(v, down).wait_recv()
                    acc_u[v] += red_u[step, v]

                @pl.when(k > 0)
                def _():
                    u_red(v, down).start()

            @pl.when(k == 0)
            def _():
                for q in (xn, yn, dn):
                    u_res(v, q).start()
                src, dst = u_part(v, p, p)
                dst[...] = src[...]

        def take(v, j):
            z_copy(v, j).wait_recv()

            @pl.when(z > 0)
            def _():
                z_copy(v, j).start()

        hats(own, hat_hi, hat_lo, p * lr)
        sigma_plane(own, p)

        def clear(v, _):
            acc_t[v] = jnp.zeros(acc_t.shape[1:], jnp.float32)
            acc_u[v] = jnp.zeros(acc_u.shape[1:], jnp.float32)
            return 0

        lax.fori_loop(z, A, clear, 0)
        each_chunk(z, build)
        for h in range(lr):
            r0 = pl.multiple_of((p * lr + h) * 2 * orb, 2 * orb)
            g_hi = hat_hi[pl.ds(r0, 2 * orb), :]
            g_lo = hat_lo[pl.ds(r0, 2 * orb), :]
            h_acc[pl.ds(h * orb, orb), :] = dot(ham_hi, g_hi, NN) + (dot(ham_hi, g_lo, NN) + dot(ham_lo, g_hi, NN))
        t_rows(z, p)

        for h in range(lr):
            arrived(xn if h % 2 == 0 else yn, h)
            onward(h).start()

        @pl.when(z + 1 < A)
        def _():
            each_chunk(z + 1, take)
            each_chunk(z + 1, build)
            t_rows(z + 1, p)

        for h in range(lr):
            arrived(yn if h % 2 == 0 else xn, h)
        for q in (xn, yn):
            hats(plane.at[step, q], hat_hi, hat_lo, q * lr)
            sigma_plane(plane.at[step, q], q)
        t_rows(z, xn, yn)

        @pl.when(z + 1 < A)
        def _():
            t_rows(z + 1, xn, yn)

        early = nj // 2

        @pl.when(z + 2 < A)
        def _():
            def one(v, j):
                @pl.when((z == 0) | (j < early))
                def _():
                    take(v, j)

                @pl.when(z == 0)
                def _():
                    build(v, j)
                    for q in (p, xn, yn):
                        t_dot(v, j, q)

            each_chunk(z + 2, one)

        for h in range(lr):
            arrived(dn, h)
        hats(plane.at[step, dn], hat_hi, hat_lo, dn * lr)
        sigma_plane(plane.at[step, dn], dn)

        t_rows(z, dn)
        t_finish(z)

        @pl.when(z + 1 < A)
        def _():
            t_rows(z + 1, dn)
            t_finish(z + 1)
            each_chunk(z + 1, u_dot)
            u_finish(z + 1)

        def late(v, _):
            done = (z == 0) & (v == z + 2)

            def one(v, j):
                @pl.when(done)
                def _():
                    t_dot(v, j, dn)

                @pl.when(jnp.logical_not(done))
                def _():
                    @pl.when((v > z + 2) | (j >= early))
                    def _():
                        take(v, j)
                    build(v, j)
                    t_dot(v, j)

                u_dot(v, j)

            each_chunk(v, one)
            t_finish(v)
            u_finish(v)
            return 0

        lax.fori_loop(z + 2, A, late, 0)

        def collect(i, _):
            w = col * ppc + i

            @pl.when(w < z)
            def _():
                part = res.at[step, w]
                remote(part, part, t_send.at[w], t_recv.at[step, w], dev(z, xn, col)).wait_recv()

            @pl.when(w > z)
            def _():
                for q in (xn, yn, dn):
                    part = res.at[step, w, :, pl.ds(pl.multiple_of(q * lr * wide, lr * wide), lr * wide)]
                    remote(part, part, u_send.at[w, q], u_recv.at[step, w, q], dev(z, xn, col)).wait_recv()

            def update(i, _):
                h, m = i // pu, i % pu
                u = (w - col * ppc) * pu + m
                r0 = pl.multiple_of(h * orb, orb)
                driven = h_acc[pl.ds(r0, orb), pl.ds(pl.multiple_of(u * wide, wide), wide)]
                driven = driven + res[step, w, pl.ds(r0, orb), pl.ds(pl.multiple_of(m * wide, wide), wide)]
                new = held[step, z, h, u] - time_step * rot(driven)

                @pl.when(step < STEPS - 1)
                def _():
                    held[step + 1, z, h, u] = new

                @pl.when(step == STEPS - 1)
                def _():
                    out[h, u] = new
                return 0

            lax.fori_loop(0, lr * pu, update, 0, unroll=UNROLL)
            return 0

        lax.fori_loop(0, ppc, collect, 0)

        for h in range(lr):
            to_x(h).wait_send()
            to_y(h).wait_send()
            onward(h).wait_send()

        def sent(v, _):
            @pl.when(z > 0)
            def _():
                each_chunk(v, lambda v, j: z_copy(v, j).wait_send())

            k = place(cz)

            @pl.when(k > 0)
            def _():
                t_red(v, down).wait_send()

            @pl.when(v > z)
            def _():
                @pl.when(k == 0)
                def _():
                    t_res(v).wait_send()

                ku = place(v // ppc)

                @pl.when(ku > 0)
                def _():
                    u_red(v, down).wait_send()

                @pl.when(ku == 0)
                def _():
                    for q in (xn, yn, dn):
                        u_res(v, q).wait_send()
            return 0

        lax.fori_loop(z, A, sent, 0)
        return 0

    lax.fori_loop(0, STEPS, step_body, 0)


def solution(mesh):
    rows, cols = mesh.shape["row"], mesh.shape["col"]
    planes = rows // GROUP

    def step(green, ham):
        lr, lc, orb, wide = green.shape
        pu = GROUP * lr
        nj = lc // min(CHUNK, lc)
        f32, bf16 = jnp.float32, jnp.bfloat16
        dma = pltpu.SemaphoreType.DMA
        big = (lr * orb, pu * wide)
        tall = (pu * orb, lr * wide)
        return pl.pallas_call(
            functools.partial(kernel, planes, cols),
            out_shape=jax.ShapeDtypeStruct(green.shape, f32),
            in_specs=[pl.BlockSpec(memory_space=pltpu.VMEM)] * 2,
            out_specs=pl.BlockSpec(memory_space=pltpu.VMEM),
            scratch_shapes=[
                pltpu.VMEM((STEPS, planes) + green.shape, f32),
                pltpu.VMEM((STEPS, GROUP) + green.shape, f32),
                pltpu.VMEM((STEPS, planes) + big, f32),
                pltpu.VMEM((STEPS, planes) + big, f32),
                pltpu.VMEM((STEPS, planes) + tall, f32),
                pltpu.VMEM((planes,) + big, f32),
                pltpu.VMEM((planes,) + tall, f32),
                pltpu.VMEM((pu * wide, lc * wide), bf16),
                pltpu.VMEM((pu * wide, lc * wide), bf16),
                pltpu.VMEM((pu * orb, lc * wide), bf16),
                pltpu.VMEM((pu * orb, lc * wide), bf16),
                pltpu.VMEM((planes, 2 * lr * orb, lc * wide), bf16),
                pltpu.VMEM((lr * wide, min(CHUNK, lc) * wide), bf16),
                pltpu.VMEM((lr * wide, min(CHUNK, lc) * wide), bf16),
                pltpu.VMEM((lr * orb, lc * wide), f32),
                dma((STEPS, planes, nj)), dma((STEPS, planes, nj)),
                dma((STEPS, lr)), dma((STEPS, lr)), dma((STEPS, lr)),
                dma((STEPS, GROUP, lr)),
                dma((planes,)), dma((STEPS, planes)),
                dma((planes,)), dma((STEPS, planes)),
                dma((planes,)), dma((STEPS, planes)),
                dma((planes, GROUP)), dma((STEPS, planes, GROUP)),
            ],
            compiler_params=pltpu.CompilerParams(
                collective_id=0, has_side_effects=True, vmem_limit_bytes=62 * 1024 * 1024
            ),
        )(green, ham)

    spec = P("row", "col", None, None)
    return jax.shard_map(step, mesh=mesh, in_specs=(spec, P()), out_specs=spec, check_vma=False)
```

```python
import functools

import jax
import jax.numpy as jnp
from jax import lax
from jax.experimental import pallas as pl
from jax.experimental.pallas import tpu as pltpu
from jax.sharding import PartitionSpec as P

STEPS = 2
time_step = 0.1

GROUP = 4
UNROLL = 8
CHUNK = 4
MESH = pl.DeviceIdType.MESH
NT = (((1,), (1,)), ((), ()))
NN = (((1,), (0,)), ((), ()))


def dot(a, b, dims):
    return lax.dot_general(a, b, dims, preferred_element_type=jnp.float32)


def split(x):
    hi = x.astype(jnp.bfloat16)
    lo = (x - hi.astype(jnp.float32)).astype(jnp.bfloat16)
    return hi, lo


def kernel(
    planes, cols, green, ham, out, held, plane, res, red_t, red_u,
    acc_t, acc_u, hat_hi, hat_lo, sig_hi, sig_lo, sx, hx_hi, hx_lo, h_acc,
    z_send, z_recv, x_send, y_send, f_send, p_recv,
    rt_send, rt_recv, ru_send, ru_recv, t_send, t_recv, u_send, u_recv,
):
    lr, lc, orb, wide = green.shape
    half = wide // 2
    B, A, C = GROUP, planes, cols
    pu = B * lr
    ppc = lc // pu
    ch = min(CHUNK, lc)
    nj = lc // ch
    kw = ch * wide

    row = lax.axis_index("row")
    col = lax.axis_index("col")
    z, p = row // B, row % B
    xn = p + 1 - 2 * (p % 2)
    yn = (p + 2) % B
    dn = (xn + 2) % B
    s_first = col * lc
    cz = z // ppc

    def dev(zz, pp, cc):
        return (zz * B + pp, cc)

    def remote(src, dst, ss, rs, to):
        return pltpu.make_async_remote_copy(
            src_ref=src, dst_ref=dst, send_sem=ss, recv_sem=rs, device_id=to, device_id_type=MESH
        )

    bar = pltpu.get_barrier_semaphore()
    for q in (xn, yn, dn):
        pl.semaphore_signal(bar, inc=1, device_id=dev(z, q, col), device_id_type=MESH)
    for k in range(1, A):
        pl.semaphore_signal(bar, inc=1, device_id=dev((z + k) % A, p, col), device_id_type=MESH)
    for k in range(1, C):
        pl.semaphore_signal(bar, inc=1, device_id=dev(z, p, (col + k) % C), device_id_type=MESH)

    lane = lax.broadcasted_iota(jnp.int32, (orb, wide), 1)
    sign = jnp.where(lane < half, jnp.float32(-1.0), jnp.float32(1.0))

    def rot(x):
        return pltpu.roll(x, half, 1) * sign

    def copy_in(i, _):
        h, m = i // lc, i % lc
        held[0, z, h, m] = green[h, m]
        return 0

    lax.fori_loop(0, lr * lc, copy_in, 0, unroll=UNROLL)
    pl.semaphore_wait(bar, (B - 1) + (A - 1) + (C - 1))

    ham_hi, ham_lo = split(ham[...])

    def needed(v, j):
        return s_first + j * ch <= (v * B + p) * lr + lr - 1

    def reached(j):
        return s_first + j * ch <= z * pu + pu - 1

    def lowered(j):
        return (z > 1) | ((z == 1) & (s_first + j * ch <= pu - 1))

    def hats(src, hi_ref, lo_ref, first):
        def one(i, _):
            h, m = i // lc, i % lc
            g = src[h, m]
            r0 = pl.multiple_of((first + h) * 2 * orb, 2 * orb)
            c0 = pl.multiple_of(m * wide, wide)
            hi, lo = split(g)
            hi_ref[pl.ds(r0, orb), pl.ds(c0, wide)] = hi
            lo_ref[pl.ds(r0, orb), pl.ds(c0, wide)] = lo
            hi, lo = split(rot(g))
            r1 = pl.multiple_of(r0 + orb, orb)
            hi_ref[pl.ds(r1, orb), pl.ds(c0, wide)] = hi
            lo_ref[pl.ds(r1, orb), pl.ds(c0, wide)] = lo
            return 0

        lax.fori_loop(0, lr * lc, one, 0, unroll=UNROLL)

    def sigma(g, t, m):
        s = s_first + m
        weight = jnp.where(s < t, jnp.float32(time_step), jnp.where(s == t, jnp.float32(0.5 * time_step), jnp.float32(0.0)))
        sq = g * g
        return split(weight * ((sq + pltpu.roll(sq, half, 1)) * g))

    def sigma_plane(src, q):
        def chunk(j, _):
            @pl.when(reached(j))
            def _():
                def one(i, _):
                    h, m = i // ch, j * ch + i % ch
                    hi, lo = sigma(src[h, m], (z * B + q) * lr + h, m)
                    r0 = pl.multiple_of((q * lr + h) * orb, orb)
                    c0 = pl.multiple_of(m * wide, wide)
                    sig_hi[pl.ds(r0, orb), pl.ds(c0, wide)] = hi
                    sig_lo[pl.ds(r0, orb), pl.ds(c0, wide)] = lo
                    return 0

                lax.fori_loop(0, lr * ch, one, 0, unroll=UNROLL)
            return 0

        lax.fori_loop(0, nj, chunk, 0)

    def step_body(step, _):
        own = held.at[step, z]

        def z_copy(v, j):
            part = held.at[step, v, :, pl.ds(j * ch, ch)]
            return remote(part, part, z_send.at[step, v, j], z_recv.at[step, v, j], dev((z + A - 1) % A, p, col))

        def each_chunk(v, action):
            def one(j, _):
                @pl.when(needed(v, j))
                def _():
                    action(v, j)
                return 0

            lax.fori_loop(0, nj, one, 0)

        def to_x(h):
            return remote(own.at[h], plane.at[step, p, h], x_send.at[step, h], p_recv.at[step, p, h], dev(z, xn, col))

        def to_y(h):
            return remote(own.at[h], plane.at[step, p, h], y_send.at[step, h], p_recv.at[step, p, h], dev(z, yn, col))

        def onward(h):
            src, to = (xn, yn) if h % 2 == 0 else (yn, xn)
            part = plane.at[step, src, h]
            return remote(part, part, f_send.at[step, h], p_recv.at[step, src, h], dev(z, to, col))

        def arrived(q, h):
            part = plane.at[step, q, h]
            remote(part, part, f_send.at[step, h], p_recv.at[step, q, h], dev(z, xn, col)).wait_recv()

        def z_down(v, j):
            @pl.when(lowered(j))
            def _():
                z_copy(v, j).start()

        def up_copy(j):
            part = held.at[step, 0, :, pl.ds(j * ch, ch)]
            return remote(part, part, z_send.at[step, 0, j], z_recv.at[step, 0, j], dev((z + 1) % A, p, col))

        def each(action):
            def one(j, _):
                action(j)
                return 0

            lax.fori_loop(0, nj, one, 0)

        each_chunk(z, z_down)
        if A > 1:
            @pl.when(z == 0)
            def _():
                each(lambda j: up_copy(j).start())

        for h in range(lr):
            to_x(h).start()
            to_y(h).start()

        def cols_of(j):
            return pl.ds(pl.multiple_of(j * kw, kw), kw)

        def build(v, j):
            def one(i, _):
                h, m = i // ch, j * ch + i % ch
                hi, lo = sigma(held[step, v, h, m], (v * B + p) * lr + h, m)
                r0 = pl.multiple_of(h * orb, orb)
                c0 = pl.multiple_of(m * wide, wide)
                sx[v, pl.ds(r0, orb), pl.ds(c0, wide)] = hi
                sx[v, pl.ds(pl.multiple_of(lr * orb + r0, orb), orb), pl.ds(c0, wide)] = lo
                return 0

            lax.fori_loop(0, lr * ch, one, 0, unroll=UNROLL)

        def t_dot(v, j, q=None):
            ks = cols_of(j)
            us = pl.ds(0, pu * wide) if q is None else pl.ds(pl.multiple_of(q * lr * wide, lr * wide), lr * wide)
            both = dot(sx[v, :, ks], hat_hi[us, ks], NT)
            low = dot(sx[v, pl.ds(0, lr * orb), ks], hat_lo[us, ks], NT)
            acc_t[v, :, us] += both[: lr * orb] + (both[lr * orb :] + low)

        def t_rows(v, *qs):
            def one(v, j):
                for q in qs:
                    t_dot(v, j, q)

            each_chunk(v, one)

        def u_dot(v, j):
            @pl.when(reached(j))
            def _():
                def one(i, _):
                    h, m = i // ch, j * ch + i % ch
                    g = held[step, v, h, m]
                    r0 = pl.multiple_of(h * 2 * orb, 2 * orb)
                    r1 = pl.multiple_of(r0 + orb, orb)
                    c0 = pl.multiple_of((i % ch) * wide, wide)
                    hi, lo = split(g)
                    hx_hi[pl.ds(r0, orb), pl.ds(c0, wide)] = hi
                    hx_lo[pl.ds(r0, orb), pl.ds(c0, wide)] = lo
                    hi, lo = split(rot(g))
                    hx_hi[pl.ds(r1, orb), pl.ds(c0, wide)] = hi
                    hx_lo[pl.ds(r1, orb), pl.ds(c0, wide)] = lo
                    return 0

                lax.fori_loop(0, lr * ch, one, 0, unroll=UNROLL)
                ks = cols_of(j)
                hi, lo = sig_hi[:, ks], sig_lo[:, ks]
                ghi, glo = hx_hi[...], hx_lo[...]
                acc_u[v] += dot(hi, ghi, NT) + (dot(hi, glo, NT) + dot(lo, ghi, NT))

        def t_red(v, to):
            return remote(acc_t.at[v], red_t.at[step, v], rt_send.at[v], rt_recv.at[step, v], dev(z, p, to))

        def u_red(v, to):
            return remote(acc_u.at[v], red_u.at[step, v], ru_send.at[v], ru_recv.at[step, v], dev(z, p, to))

        def t_res(v):
            return remote(acc_t.at[v], res.at[step, z], t_send.at[v], t_recv.at[step, z], dev(v, p, col))

        def u_part(v, q, at):
            return (
                acc_u.at[v, pl.ds(pl.multiple_of(q * lr * orb, lr * orb), lr * orb), :],
                res.at[step, v, :, pl.ds(pl.multiple_of(at * lr * wide, lr * wide), lr * wide)],
            )

        def u_res(v, q):
            src, dst = u_part(v, q, p)
            return remote(src, dst, u_send.at[v, q], u_recv.at[step, v, p], dev(z, q, col))

        def place(owner):
            return (col + C - owner) % C

        down = (col + C - 1) % C

        def t_finish(v):
            k = place(cz)
            if C > 1:
                @pl.when(k > 0)
                def _():
                    if C > 2:
                        @pl.when(k < C - 1)
                        def _():
                            t_red(v, down).wait_recv()
                            acc_t[v] += red_t[step, v]

                    t_red(v, down).start()

            @pl.when(k == 0)
            def _():
                if C > 1:
                    t_red(v, down).wait_recv()

                @pl.when(v > z)
                def _():
                    if C > 1:
                        acc_t[v] += red_t[step, v]
                    t_res(v).start()

                @pl.when(v == z)
                def _():
                    if C > 1:
                        res[step, z] = acc_t[z] + red_t[step, z]
                    else:
                        res[step, z] = acc_t[z]

        def u_finish(v):
            k = place(v // ppc)
            if C > 1:
                @pl.when(k < C - 1)
                def _():
                    u_red(v, down).wait_recv()
                    acc_u[v] += red_u[step, v]

                @pl.when(k > 0)
                def _():
                    u_red(v, down).start()

            @pl.when(k == 0)
            def _():
                for q in (xn, yn, dn):
                    u_res(v, q).start()
                src, dst = u_part(v, p, p)
                dst[...] = src[...]

        def take(v, j):
            z_copy(v, j).wait_recv()
            z_down(v, j)

        def take_up(j):
            up_copy(j).wait_recv()

            @pl.when(z + 1 < A)
            def _():
                up_copy(j).start()

        hats(own, hat_hi, hat_lo, p * lr)
        sigma_plane(own, p)

        def clear(v, _):
            acc_t[v] = jnp.zeros(acc_t.shape[1:], jnp.float32)
            acc_u[v] = jnp.zeros(acc_u.shape[1:], jnp.float32)
            return 0

        lax.fori_loop(z, A, clear, 0)
        acc_u[0] = jnp.zeros(acc_u.shape[1:], jnp.float32)
        each_chunk(z, build)
        for h in range(lr):
            r0 = pl.multiple_of((p * lr + h) * 2 * orb, 2 * orb)
            g_hi = hat_hi[pl.ds(r0, 2 * orb), :]
            g_lo = hat_lo[pl.ds(r0, 2 * orb), :]
            h_acc[pl.ds(h * orb, orb), :] = dot(ham_hi, g_hi, NN) + (dot(ham_hi, g_lo, NN) + dot(ham_lo, g_hi, NN))
        t_rows(z, p)

        for h in range(lr):
            arrived(xn if h % 2 == 0 else yn, h)
            onward(h).start()

        above = (z > 0) & (z + 1 < A)

        @pl.when(above)
        def _():
            each_chunk(z + 1, take)

        @pl.when(z > 0)
        def _():
            each(take_up)

        @pl.when(above)
        def _():
            each_chunk(z + 1, build)
            t_rows(z + 1, p)

        for h in range(lr):
            arrived(yn if h % 2 == 0 else xn, h)
        for q in (xn, yn):
            hats(plane.at[step, q], hat_hi, hat_lo, q * lr)
            sigma_plane(plane.at[step, q], q)
        t_rows(z, xn, yn)

        @pl.when(above)
        def _():
            t_rows(z + 1, xn, yn)

        early = nj // 2

        @pl.when((z > 0) & (z + 2 < A))
        def _():
            def one(v, j):
                @pl.when(j < early)
                def _():
                    take(v, j)
                    build(v, j)
                    for q in (p, xn, yn):
                        t_dot(v, j, q)

            each_chunk(z + 2, one)

        for h in range(lr):
            arrived(dn, h)
        hats(plane.at[step, dn], hat_hi, hat_lo, dn * lr)
        sigma_plane(plane.at[step, dn], dn)

        t_rows(z, dn)
        t_finish(z)

        @pl.when(above)
        def _():
            t_rows(z + 1, dn)
            t_finish(z + 1)
            each_chunk(z + 1, u_dot)
            u_finish(z + 1)

        def late(v, _):
            def one(v, j):
                done = (v == z + 2) & (j < early)

                @pl.when(done)
                def _():
                    t_dot(v, j, dn)

                @pl.when(jnp.logical_not(done))
                def _():
                    take(v, j)
                    build(v, j)
                    t_dot(v, j)

                u_dot(v, j)

            each_chunk(v, one)
            t_finish(v)
            u_finish(v)
            return 0

        @pl.when(z > 0)
        def _():
            lax.fori_loop(z + 2, A, late, 0)
            each(lambda j: u_dot(0, j))
            u_finish(0)

        @pl.when(z == 0)
        def _():
            def lowest(v, _):
                def one(j):
                    @pl.when(reached(j))
                    def _():
                        take(v, j)
                        u_dot(v, j)

                each(one)
                u_finish(v)
                return 0

            lax.fori_loop(1, A, lowest, 0)

        def collect(i, _):
            w = col * ppc + i

            in_plane = (w > z) | ((w == 0) & (z > 0))

            @pl.when((w < z) & (w > 0))
            def _():
                part = res.at[step, w]
                remote(part, part, t_send.at[w], t_recv.at[step, w], dev(z, xn, col)).wait_recv()

            @pl.when(in_plane)
            def _():
                for q in (xn, yn, dn):
                    part = res.at[step, w, :, pl.ds(pl.multiple_of(q * lr * wide, lr * wide), lr * wide)]
                    remote(part, part, u_send.at[w, q], u_recv.at[step, w, q], dev(z, xn, col)).wait_recv()

            def update(i, _):
                h, m = i // pu, i % pu
                u = (w - col * ppc) * pu + m
                r0 = pl.multiple_of(h * orb, orb)
                driven = h_acc[pl.ds(r0, orb), pl.ds(pl.multiple_of(u * wide, wide), wide)]
                driven = driven + res[step, w, pl.ds(r0, orb), pl.ds(pl.multiple_of(m * wide, wide), wide)]
                new = held[step, z, h, u] - time_step * rot(driven)

                @pl.when(step < STEPS - 1)
                def _():
                    held[step + 1, z, h, u] = new

                @pl.when(step == STEPS - 1)
                def _():
                    out[h, u] = new
                return 0

            lax.fori_loop(0, lr * pu, update, 0, unroll=UNROLL)
            return 0

        lax.fori_loop(0, ppc, collect, 0)

        for h in range(lr):
            to_x(h).wait_send()
            to_y(h).wait_send()
            onward(h).wait_send()

        def u_sent(v):
            ku = place(v // ppc)

            @pl.when(ku > 0)
            def _():
                u_red(v, down).wait_send()

            @pl.when(ku == 0)
            def _():
                for q in (xn, yn, dn):
                    u_res(v, q).wait_send()

        def left(v, j):
            @pl.when(lowered(j))
            def _():
                z_copy(v, j).wait_send()

        def sent(v, _):
            each_chunk(v, left)

            @pl.when((v == z) | (z > 0))
            def _():
                k = place(cz)

                @pl.when(k > 0)
                def _():
                    t_red(v, down).wait_send()

                @pl.when((k == 0) & (v > z))
                def _():
                    t_res(v).wait_send()

            @pl.when(v > z)
            def _():
                u_sent(v)
            return 0

        @pl.when(z > 0)
        def _():
            u_sent(0)

        if A > 1:
            @pl.when(z + 1 < A)
            def _():
                each(lambda j: up_copy(j).wait_send())

        lax.fori_loop(z, A, sent, 0)
        return 0

    lax.fori_loop(0, STEPS, step_body, 0)


def solution(mesh):
    rows, cols = mesh.shape["row"], mesh.shape["col"]
    planes = rows // GROUP

    def step(green, ham):
        lr, lc, orb, wide = green.shape
        pu = GROUP * lr
        nj = lc // min(CHUNK, lc)
        f32, bf16 = jnp.float32, jnp.bfloat16
        dma = pltpu.SemaphoreType.DMA
        big = (lr * orb, pu * wide)
        tall = (pu * orb, lr * wide)
        return pl.pallas_call(
            functools.partial(kernel, planes, cols),
            out_shape=jax.ShapeDtypeStruct(green.shape, f32),
            in_specs=[pl.BlockSpec(memory_space=pltpu.VMEM)] * 2,
            out_specs=pl.BlockSpec(memory_space=pltpu.VMEM),
            scratch_shapes=[
                pltpu.VMEM((STEPS, planes) + green.shape, f32),
                pltpu.VMEM((STEPS, GROUP) + green.shape, f32),
                pltpu.VMEM((STEPS, planes) + big, f32),
                pltpu.VMEM((STEPS, planes) + big, f32),
                pltpu.VMEM((STEPS, planes) + tall, f32),
                pltpu.VMEM((planes,) + big, f32),
                pltpu.VMEM((planes,) + tall, f32),
                pltpu.VMEM((pu * wide, lc * wide), bf16),
                pltpu.VMEM((pu * wide, lc * wide), bf16),
                pltpu.VMEM((pu * orb, lc * wide), bf16),
                pltpu.VMEM((pu * orb, lc * wide), bf16),
                pltpu.VMEM((planes, 2 * lr * orb, lc * wide), bf16),
                pltpu.VMEM((lr * wide, min(CHUNK, lc) * wide), bf16),
                pltpu.VMEM((lr * wide, min(CHUNK, lc) * wide), bf16),
                pltpu.VMEM((lr * orb, lc * wide), f32),
                dma((STEPS, planes, nj)), dma((STEPS, planes, nj)),
                dma((STEPS, lr)), dma((STEPS, lr)), dma((STEPS, lr)),
                dma((STEPS, GROUP, lr)),
                dma((planes,)), dma((STEPS, planes)),
                dma((planes,)), dma((STEPS, planes)),
                dma((planes,)), dma((STEPS, planes)),
                dma((planes, GROUP)), dma((STEPS, planes, GROUP)),
            ],
            compiler_params=pltpu.CompilerParams(
                collective_id=0, has_side_effects=True, vmem_limit_bytes=62 * 1024 * 1024
            ),
        )(green, ham)

    spec = P("row", "col", None, None)
    return jax.shard_map(step, mesh=mesh, in_specs=(spec, P()), out_specs=spec, check_vma=False)
```

```python
import functools

import jax
import jax.numpy as jnp
from jax import lax
from jax.experimental import pallas as pl
from jax.experimental.pallas import tpu as pltpu
from jax.sharding import PartitionSpec as P

STEPS = 2
time_step = 0.1

GROUP = 4
UNROLL = 8
CHUNK = 4
MESH = pl.DeviceIdType.MESH
NT = (((1,), (1,)), ((), ()))
NN = (((1,), (0,)), ((), ()))


def dot(a, b, dims):
    return lax.dot_general(a, b, dims, preferred_element_type=jnp.float32)


def split(x):
    hi = x.astype(jnp.bfloat16)
    lo = (x - hi.astype(jnp.float32)).astype(jnp.bfloat16)
    return hi, lo


def kernel(
    planes, cols, green, ham, out, held, plane, res, red_t, red_u,
    acc_t, acc_u, hat_hi, hat_lo, sig_hi, sig_lo, sx, hx_hi, hx_lo, h_acc,
    z_send, z_recv, x_send, y_send, f_send, p_recv,
    rt_send, rt_recv, ru_send, ru_recv, t_send, t_recv, u_send, u_recv,
):
    lr, lc, orb, wide = green.shape
    half = wide // 2
    B, A, C = GROUP, planes, cols
    pu = B * lr
    ppc = lc // pu
    ch = min(CHUNK, lc)
    nj = lc // ch
    kw = ch * wide

    row = lax.axis_index("row")
    col = lax.axis_index("col")
    z, p = row // B, row % B
    xn = p + 1 - 2 * (p % 2)
    yn = (p + 2) % B
    dn = (xn + 2) % B
    s_first = col * lc
    cz = z // ppc

    def dev(zz, pp, cc):
        return (zz * B + pp, cc)

    def remote(src, dst, ss, rs, to):
        return pltpu.make_async_remote_copy(
            src_ref=src, dst_ref=dst, send_sem=ss, recv_sem=rs, device_id=to, device_id_type=MESH
        )

    bar = pltpu.get_barrier_semaphore()
    for q in (xn, yn, dn):
        pl.semaphore_signal(bar, inc=1, device_id=dev(z, q, col), device_id_type=MESH)
    for k in range(1, A):
        pl.semaphore_signal(bar, inc=1, device_id=dev((z + k) % A, p, col), device_id_type=MESH)
    for k in range(1, C):
        pl.semaphore_signal(bar, inc=1, device_id=dev(z, p, (col + k) % C), device_id_type=MESH)

    lane = lax.broadcasted_iota(jnp.int32, (orb, wide), 1)
    sign = jnp.where(lane < half, jnp.float32(-1.0), jnp.float32(1.0))

    def rot(x):
        return pltpu.roll(x, half, 1) * sign

    def copy_in(i, _):
        h, m = i // lc, i % lc
        held[0, z, h, m] = green[h, m]
        return 0

    lax.fori_loop(0, lr * lc, copy_in, 0, unroll=UNROLL)
    pl.semaphore_wait(bar, (B - 1) + (A - 1) + (C - 1))

    ham_hi, ham_lo = split(ham[...])

    def needed(v, j):
        return s_first + j * ch <= (v * B + p) * lr + lr - 1

    def reached(j):
        return s_first + j * ch <= z * pu + pu - 1

    def lowered(j):
        return (z > 1) | ((z == 1) & (s_first + j * ch <= pu - 1))

    def hats(src, hi_ref, lo_ref, first):
        def one(i, _):
            h, m = i // lc, i % lc
            g = src[h, m]
            r0 = pl.multiple_of((first + h) * 2 * orb, 2 * orb)
            c0 = pl.multiple_of(m * wide, wide)
            hi, lo = split(g)
            hi_ref[pl.ds(r0, orb), pl.ds(c0, wide)] = hi
            lo_ref[pl.ds(r0, orb), pl.ds(c0, wide)] = lo
            hi, lo = split(rot(g))
            r1 = pl.multiple_of(r0 + orb, orb)
            hi_ref[pl.ds(r1, orb), pl.ds(c0, wide)] = hi
            lo_ref[pl.ds(r1, orb), pl.ds(c0, wide)] = lo
            return 0

        lax.fori_loop(0, lr * lc, one, 0, unroll=UNROLL)

    def sigma(g, t, m):
        s = s_first + m
        weight = jnp.where(s < t, jnp.float32(time_step), jnp.where(s == t, jnp.float32(0.5 * time_step), jnp.float32(0.0)))
        sq = g * g
        return split(weight * ((sq + pltpu.roll(sq, half, 1)) * g))

    def sigma_plane(src, q):
        def chunk(j, _):
            @pl.when(reached(j))
            def _():
                def one(i, _):
                    h, m = i // ch, j * ch + i % ch
                    hi, lo = sigma(src[h, m], (z * B + q) * lr + h, m)
                    r0 = pl.multiple_of((q * lr + h) * orb, orb)
                    c0 = pl.multiple_of(m * wide, wide)
                    sig_hi[pl.ds(r0, orb), pl.ds(c0, wide)] = hi
                    sig_lo[pl.ds(r0, orb), pl.ds(c0, wide)] = lo
                    return 0

                lax.fori_loop(0, lr * ch, one, 0, unroll=UNROLL)
            return 0

        lax.fori_loop(0, nj, chunk, 0)

    def step_body(step, _):
        own = held.at[step, z]

        def z_copy(v, j):
            part = held.at[step, v, :, pl.ds(j * ch, ch)]
            return remote(part, part, z_send.at[step, v, j], z_recv.at[step, v, j], dev((z + A - 1) % A, p, col))

        def each_chunk(v, action):
            def one(j, _):
                @pl.when(needed(v, j))
                def _():
                    action(v, j)
                return 0

            lax.fori_loop(0, nj, one, 0)

        def to_x(h):
            return remote(own.at[h], plane.at[step, p, h], x_send.at[step, h], p_recv.at[step, p, h], dev(z, xn, col))

        def to_y(h):
            return remote(own.at[h], plane.at[step, p, h], y_send.at[step, h], p_recv.at[step, p, h], dev(z, yn, col))

        def onward(h):
            src, to = (xn, yn) if h % 2 == 0 else (yn, xn)
            part = plane.at[step, src, h]
            return remote(part, part, f_send.at[step, h], p_recv.at[step, src, h], dev(z, to, col))

        def arrived(q, h):
            part = plane.at[step, q, h]
            remote(part, part, f_send.at[step, h], p_recv.at[step, q, h], dev(z, xn, col)).wait_recv()

        def z_down(v, j):
            @pl.when(lowered(j))
            def _():
                z_copy(v, j).start()

        def up_copy(j):
            part = held.at[step, 0, :, pl.ds(j * ch, ch)]
            return remote(part, part, z_send.at[step, 0, j], z_recv.at[step, 0, j], dev((z + 1) % A, p, col))

        def each(action):
            def one(j, _):
                action(j)
                return 0

            lax.fori_loop(0, nj, one, 0)

        each_chunk(z, z_down)
        if A > 1:
            @pl.when(z == 0)
            def _():
                each(lambda j: up_copy(j).start())

        for h in range(lr):
            to_x(h).start()
            to_y(h).start()

        def cols_of(j):
            return pl.ds(pl.multiple_of(j * kw, kw), kw)

        def build(v, j):
            def one(i, _):
                h, m = i // ch, j * ch + i % ch
                hi, lo = sigma(held[step, v, h, m], (v * B + p) * lr + h, m)
                r0 = pl.multiple_of(h * orb, orb)
                c0 = pl.multiple_of(m * wide, wide)
                sx[v, pl.ds(r0, orb), pl.ds(c0, wide)] = hi
                sx[v, pl.ds(pl.multiple_of(lr * orb + r0, orb), orb), pl.ds(c0, wide)] = lo
                return 0

            lax.fori_loop(0, lr * ch, one, 0, unroll=UNROLL)

        def t_dot(v, j, q=None):
            ks = cols_of(j)
            us = pl.ds(0, pu * wide) if q is None else pl.ds(pl.multiple_of(q * lr * wide, lr * wide), lr * wide)
            both = dot(sx[v, :, ks], hat_hi[us, ks], NT)
            low = dot(sx[v, pl.ds(0, lr * orb), ks], hat_lo[us, ks], NT)
            acc_t[v, :, us] += both[: lr * orb] + (both[lr * orb :] + low)

        def t_rows(v, *qs):
            def one(v, j):
                for q in qs:
                    t_dot(v, j, q)

            each_chunk(v, one)

        def u_dot(v, j):
            @pl.when(reached(j))
            def _():
                def one(i, _):
                    h, m = i // ch, j * ch + i % ch
                    g = held[step, v, h, m]
                    r0 = pl.multiple_of(h * 2 * orb, 2 * orb)
                    r1 = pl.multiple_of(r0 + orb, orb)
                    c0 = pl.multiple_of((i % ch) * wide, wide)
                    hi, lo = split(g)
                    hx_hi[pl.ds(r0, orb), pl.ds(c0, wide)] = hi
                    hx_lo[pl.ds(r0, orb), pl.ds(c0, wide)] = lo
                    hi, lo = split(rot(g))
                    hx_hi[pl.ds(r1, orb), pl.ds(c0, wide)] = hi
                    hx_lo[pl.ds(r1, orb), pl.ds(c0, wide)] = lo
                    return 0

                lax.fori_loop(0, lr * ch, one, 0, unroll=UNROLL)
                ks = cols_of(j)
                hi, lo = sig_hi[:, ks], sig_lo[:, ks]
                ghi, glo = hx_hi[...], hx_lo[...]
                acc_u[v] += dot(hi, ghi, NT) + (dot(hi, glo, NT) + dot(lo, ghi, NT))

        def t_red(v, to):
            return remote(acc_t.at[v], red_t.at[step, v], rt_send.at[v], rt_recv.at[step, v], dev(z, p, to))

        def u_red(v, to):
            return remote(acc_u.at[v], red_u.at[step, v], ru_send.at[v], ru_recv.at[step, v], dev(z, p, to))

        def t_res(v):
            return remote(acc_t.at[v], res.at[step, z], t_send.at[v], t_recv.at[step, z], dev(v, p, col))

        def u_part(v, q, at):
            return (
                acc_u.at[v, pl.ds(pl.multiple_of(q * lr * orb, lr * orb), lr * orb), :],
                res.at[step, v, :, pl.ds(pl.multiple_of(at * lr * wide, lr * wide), lr * wide)],
            )

        def u_res(v, q):
            src, dst = u_part(v, q, p)
            return remote(src, dst, u_send.at[v, q], u_recv.at[step, v, p], dev(z, q, col))

        def place(owner):
            return (col + C - owner) % C

        down = (col + C - 1) % C

        def t_finish(v):
            k = place(cz)
            if C > 1:
                @pl.when(k > 0)
                def _():
                    if C > 2:
                        @pl.when(k < C - 1)
                        def _():
                            t_red(v, down).wait_recv()
                            acc_t[v] += red_t[step, v]

                    t_red(v, down).start()

            @pl.when(k == 0)
            def _():
                if C > 1:
                    t_red(v, down).wait_recv()

                @pl.when(v > z)
                def _():
                    if C > 1:
                        acc_t[v] += red_t[step, v]
                    t_res(v).start()

                @pl.when(v == z)
                def _():
                    if C > 1:
                        res[step, z] = acc_t[z] + red_t[step, z]
                    else:
                        res[step, z] = acc_t[z]

        def u_finish(v):
            k = place(v // ppc)
            if C > 1:
                @pl.when(k < C - 1)
                def _():
                    u_red(v, down).wait_recv()
                    acc_u[v] += red_u[step, v]

                @pl.when(k > 0)
                def _():
                    u_red(v, down).start()

            @pl.when(k == 0)
            def _():
                for q in (xn, yn, dn):
                    u_res(v, q).start()
                src, dst = u_part(v, p, p)
                dst[...] = src[...]

        def take(v, j):
            z_copy(v, j).wait_recv()
            z_down(v, j)

        def take_up(j):
            up_copy(j).wait_recv()

            @pl.when(z + 1 < A)
            def _():
                up_copy(j).start()

        above = (z > 0) & (z + 1 < A)

        def pass_on(j):
            @pl.when(above)
            def _():
                take_up(j)

                @pl.when(needed(z + 1, j))
                def _():
                    take(z + 1, j)

        def clear(v, _):
            acc_t[v] = jnp.zeros(acc_t.shape[1:], jnp.float32)
            acc_u[v] = jnp.zeros(acc_u.shape[1:], jnp.float32)
            return 0

        def prepare():
            sigma_plane(own, p)
            lax.fori_loop(z, A, clear, 0)
            acc_u[0] = jnp.zeros(acc_u.shape[1:], jnp.float32)

        def one_body():
            each_chunk(z, build)
            for h in range(lr):
                r0 = pl.multiple_of((p * lr + h) * 2 * orb, 2 * orb)
                g_hi = hat_hi[pl.ds(r0, 2 * orb), :]
                g_lo = hat_lo[pl.ds(r0, 2 * orb), :]
                h_acc[pl.ds(h * orb, orb), :] = dot(ham_hi, g_hi, NN) + (dot(ham_hi, g_lo, NN) + dot(ham_lo, g_hi, NN))
            t_rows(z, p)

        def neighbours():
            for h in range(lr):
                arrived(xn if h % 2 == 0 else yn, h)
                onward(h).start()

        hats(own, hat_hi, hat_lo, p * lr)
        work = [prepare, one_body, neighbours]
        for j in range(max(nj, len(work))):
            if j < nj:
                pass_on(j)
            if j < len(work):
                work[j]()

        @pl.when(above)
        def _():
            each_chunk(z + 1, build)
            t_rows(z + 1, p)

        for h in range(lr):
            arrived(yn if h % 2 == 0 else xn, h)
        for q in (xn, yn):
            hats(plane.at[step, q], hat_hi, hat_lo, q * lr)
            sigma_plane(plane.at[step, q], q)
        t_rows(z, xn, yn)

        @pl.when(above)
        def _():
            t_rows(z + 1, xn, yn)

        early = nj // 2

        @pl.when((z > 0) & (z + 2 < A))
        def _():
            def one(v, j):
                @pl.when(j < early)
                def _():
                    take(v, j)
                    build(v, j)
                    for q in (p, xn, yn):
                        t_dot(v, j, q)

            each_chunk(z + 2, one)

        for h in range(lr):
            arrived(dn, h)
        hats(plane.at[step, dn], hat_hi, hat_lo, dn * lr)
        sigma_plane(plane.at[step, dn], dn)

        t_rows(z, dn)
        t_finish(z)

        @pl.when(above)
        def _():
            t_rows(z + 1, dn)
            t_finish(z + 1)
            each_chunk(z + 1, u_dot)
            u_finish(z + 1)

        def late(v, _):
            def one(v, j):
                done = (v == z + 2) & (j < early)

                @pl.when(done)
                def _():
                    t_dot(v, j, dn)

                @pl.when(jnp.logical_not(done))
                def _():
                    take(v, j)
                    build(v, j)
                    t_dot(v, j)

                u_dot(v, j)

            each_chunk(v, one)
            t_finish(v)
            u_finish(v)
            return 0

        @pl.when(z > 0)
        def _():
            lax.fori_loop(z + 2, A, late, 0)
            @pl.when(z + 1 == A)
            def _():
                each(take_up)

            each(lambda j: u_dot(0, j))
            u_finish(0)

        @pl.when(z == 0)
        def _():
            def lowest(v, _):
                def one(j):
                    @pl.when(reached(j))
                    def _():
                        take(v, j)
                        u_dot(v, j)

                each(one)
                u_finish(v)
                return 0

            lax.fori_loop(1, A, lowest, 0)

        def collect(i, _):
            w = col * ppc + i

            in_plane = (w > z) | ((w == 0) & (z > 0))

            @pl.when((w < z) & (w > 0))
            def _():
                part = res.at[step, w]
                remote(part, part, t_send.at[w], t_recv.at[step, w], dev(z, xn, col)).wait_recv()

            @pl.when(in_plane)
            def _():
                for q in (xn, yn, dn):
                    part = res.at[step, w, :, pl.ds(pl.multiple_of(q * lr * wide, lr * wide), lr * wide)]
                    remote(part, part, u_send.at[w, q], u_recv.at[step, w, q], dev(z, xn, col)).wait_recv()

            def update(i, _):
                h, m = i // pu, i % pu
                u = (w - col * ppc) * pu + m
                r0 = pl.multiple_of(h * orb, orb)
                driven = h_acc[pl.ds(r0, orb), pl.ds(pl.multiple_of(u * wide, wide), wide)]
                driven = driven + res[step, w, pl.ds(r0, orb), pl.ds(pl.multiple_of(m * wide, wide), wide)]
                new = held[step, z, h, u] - time_step * rot(driven)

                @pl.when(step < STEPS - 1)
                def _():
                    held[step + 1, z, h, u] = new

                @pl.when(step == STEPS - 1)
                def _():
                    out[h, u] = new
                return 0

            lax.fori_loop(0, lr * pu, update, 0, unroll=UNROLL)
            return 0

        lax.fori_loop(0, ppc, collect, 0)

        for h in range(lr):
            to_x(h).wait_send()
            to_y(h).wait_send()
            onward(h).wait_send()

        def u_sent(v):
            ku = place(v // ppc)

            @pl.when(ku > 0)
            def _():
                u_red(v, down).wait_send()

            @pl.when(ku == 0)
            def _():
                for q in (xn, yn, dn):
                    u_res(v, q).wait_send()

        def left(v, j):
            @pl.when(lowered(j))
            def _():
                z_copy(v, j).wait_send()

        def sent(v, _):
            each_chunk(v, left)

            @pl.when((v == z) | (z > 0))
            def _():
                k = place(cz)

                @pl.when(k > 0)
                def _():
                    t_red(v, down).wait_send()

                @pl.when((k == 0) & (v > z))
                def _():
                    t_res(v).wait_send()

            @pl.when(v > z)
            def _():
                u_sent(v)
            return 0

        @pl.when(z > 0)
        def _():
            u_sent(0)

        if A > 1:
            @pl.when(z + 1 < A)
            def _():
                each(lambda j: up_copy(j).wait_send())

        lax.fori_loop(z, A, sent, 0)
        return 0

    lax.fori_loop(0, STEPS, step_body, 0)


def solution(mesh):
    rows, cols = mesh.shape["row"], mesh.shape["col"]
    planes = rows // GROUP

    def step(green, ham):
        lr, lc, orb, wide = green.shape
        pu = GROUP * lr
        nj = lc // min(CHUNK, lc)
        f32, bf16 = jnp.float32, jnp.bfloat16
        dma = pltpu.SemaphoreType.DMA
        big = (lr * orb, pu * wide)
        tall = (pu * orb, lr * wide)
        return pl.pallas_call(
            functools.partial(kernel, planes, cols),
            out_shape=jax.ShapeDtypeStruct(green.shape, f32),
            in_specs=[pl.BlockSpec(memory_space=pltpu.VMEM)] * 2,
            out_specs=pl.BlockSpec(memory_space=pltpu.VMEM),
            scratch_shapes=[
                pltpu.VMEM((STEPS, planes) + green.shape, f32),
                pltpu.VMEM((STEPS, GROUP) + green.shape, f32),
                pltpu.VMEM((STEPS, planes) + big, f32),
                pltpu.VMEM((STEPS, planes) + big, f32),
                pltpu.VMEM((STEPS, planes) + tall, f32),
                pltpu.VMEM((planes,) + big, f32),
                pltpu.VMEM((planes,) + tall, f32),
                pltpu.VMEM((pu * wide, lc * wide), bf16),
                pltpu.VMEM((pu * wide, lc * wide), bf16),
                pltpu.VMEM((pu * orb, lc * wide), bf16),
                pltpu.VMEM((pu * orb, lc * wide), bf16),
                pltpu.VMEM((planes, 2 * lr * orb, lc * wide), bf16),
                pltpu.VMEM((lr * wide, min(CHUNK, lc) * wide), bf16),
                pltpu.VMEM((lr * wide, min(CHUNK, lc) * wide), bf16),
                pltpu.VMEM((lr * orb, lc * wide), f32),
                dma((STEPS, planes, nj)), dma((STEPS, planes, nj)),
                dma((STEPS, lr)), dma((STEPS, lr)), dma((STEPS, lr)),
                dma((STEPS, GROUP, lr)),
                dma((planes,)), dma((STEPS, planes)),
                dma((planes,)), dma((STEPS, planes)),
                dma((planes,)), dma((STEPS, planes)),
                dma((planes, GROUP)), dma((STEPS, planes, GROUP)),
            ],
            compiler_params=pltpu.CompilerParams(
                collective_id=0, has_side_effects=True, vmem_limit_bytes=62 * 1024 * 1024
            ),
        )(green, ham)

    spec = P("row", "col", None, None)
    return jax.shard_map(step, mesh=mesh, in_specs=(spec, P()), out_specs=spec, check_vma=False)
```

```python
import functools

import jax
import jax.numpy as jnp
from jax import lax
from jax.experimental import pallas as pl
from jax.experimental.pallas import tpu as pltpu
from jax.sharding import PartitionSpec as P

STEPS = 2
time_step = 0.1

GROUP = 4
UNROLL = 8
CHUNK = 4
MESH = pl.DeviceIdType.MESH
NT = (((1,), (1,)), ((), ()))
NN = (((1,), (0,)), ((), ()))


def dot(a, b, dims):
    return lax.dot_general(a, b, dims, preferred_element_type=jnp.float32)


def split(x):
    hi = x.astype(jnp.bfloat16)
    lo = (x - hi.astype(jnp.float32)).astype(jnp.bfloat16)
    return hi, lo


def kernel(
    planes, cols, green, ham, out, held, plane, res, red_t, red_u,
    acc_t, acc_u, hat_hi, hat_lo, sig_hi, sig_lo, sx, hx_hi, hx_lo, h_acc,
    z_send, z_recv, x_send, y_send, f_send, p_recv,
    rt_send, rt_recv, ru_send, ru_recv, t_send, t_recv, u_send, u_recv,
):
    lr, lc, orb, wide = green.shape
    half = wide // 2
    B, A, C = GROUP, planes, cols
    pu = B * lr
    ppc = lc // pu
    ch = min(CHUNK, lc)
    nj = lc // ch
    kw = ch * wide

    row = lax.axis_index("row")
    col = lax.axis_index("col")
    z, p = row // B, row % B
    xn = p + 1 - 2 * (p % 2)
    yn = (p + 2) % B
    dn = (xn + 2) % B
    s_first = col * lc
    cz = z // ppc

    def dev(zz, pp, cc):
        return (zz * B + pp, cc)

    def remote(src, dst, ss, rs, to):
        return pltpu.make_async_remote_copy(
            src_ref=src, dst_ref=dst, send_sem=ss, recv_sem=rs, device_id=to, device_id_type=MESH
        )

    bar = pltpu.get_barrier_semaphore()
    for q in (xn, yn, dn):
        pl.semaphore_signal(bar, inc=1, device_id=dev(z, q, col), device_id_type=MESH)
    for k in range(1, A):
        pl.semaphore_signal(bar, inc=1, device_id=dev((z + k) % A, p, col), device_id_type=MESH)
    for k in range(1, C):
        pl.semaphore_signal(bar, inc=1, device_id=dev(z, p, (col + k) % C), device_id_type=MESH)

    lane = lax.broadcasted_iota(jnp.int32, (orb, wide), 1)
    sign = jnp.where(lane < half, jnp.float32(-1.0), jnp.float32(1.0))

    def rot(x):
        return pltpu.roll(x, half, 1) * sign

    def copy_in(i, _):
        h, m = i // lc, i % lc
        held[0, z, h, m] = green[h, m]
        return 0

    lax.fori_loop(0, lr * lc, copy_in, 0, unroll=UNROLL)
    pl.semaphore_wait(bar, (B - 1) + (A - 1) + (C - 1))

    ham_hi, ham_lo = split(ham[...])

    def needed(v, j):
        return s_first + j * ch <= (v * B + p) * lr + lr - 1

    def reached(j):
        return s_first + j * ch <= z * pu + pu - 1

    def lowered(j):
        return (z > 1) | ((z == 1) & (s_first + j * ch <= pu - 1))

    def hats(src, hi_ref, lo_ref, first):
        def one(i, _):
            h, m = i // lc, i % lc
            g = src[h, m]
            r0 = pl.multiple_of((first + h) * 2 * orb, 2 * orb)
            c0 = pl.multiple_of(m * wide, wide)
            hi, lo = split(g)
            hi_ref[pl.ds(r0, orb), pl.ds(c0, wide)] = hi
            lo_ref[pl.ds(r0, orb), pl.ds(c0, wide)] = lo
            hi, lo = split(rot(g))
            r1 = pl.multiple_of(r0 + orb, orb)
            hi_ref[pl.ds(r1, orb), pl.ds(c0, wide)] = hi
            lo_ref[pl.ds(r1, orb), pl.ds(c0, wide)] = lo
            return 0

        lax.fori_loop(0, lr * lc, one, 0, unroll=UNROLL)

    def sigma(g, t, m):
        s = s_first + m
        weight = jnp.where(s < t, jnp.float32(time_step), jnp.where(s == t, jnp.float32(0.5 * time_step), jnp.float32(0.0)))
        sq = g * g
        return split(weight * ((sq + pltpu.roll(sq, half, 1)) * g))

    def sigma_plane(src, q):
        def chunk(j, _):
            @pl.when(reached(j))
            def _():
                def one(i, _):
                    h, m = i // ch, j * ch + i % ch
                    hi, lo = sigma(src[h, m], (z * B + q) * lr + h, m)
                    r0 = pl.multiple_of((q * lr + h) * orb, orb)
                    c0 = pl.multiple_of(m * wide, wide)
                    sig_hi[pl.ds(r0, orb), pl.ds(c0, wide)] = hi
                    sig_lo[pl.ds(r0, orb), pl.ds(c0, wide)] = lo
                    return 0

                lax.fori_loop(0, lr * ch, one, 0, unroll=UNROLL)
            return 0

        lax.fori_loop(0, nj, chunk, 0)

    def step_body(step, _):
        own = held.at[step, z]

        def z_copy(v, j):
            part = held.at[step, v, :, pl.ds(j * ch, ch)]
            return remote(part, part, z_send.at[step, v, j], z_recv.at[step, v, j], dev((z + A - 1) % A, p, col))

        def each_chunk(v, action):
            def one(j, _):
                @pl.when(needed(v, j))
                def _():
                    action(v, j)
                return 0

            lax.fori_loop(0, nj, one, 0)

        def to_x(h):
            return remote(own.at[h], plane.at[step, p, h], x_send.at[step, h], p_recv.at[step, p, h], dev(z, xn, col))

        def to_y(h):
            return remote(own.at[h], plane.at[step, p, h], y_send.at[step, h], p_recv.at[step, p, h], dev(z, yn, col))

        def onward(h):
            src, to = (xn, yn) if h % 2 == 0 else (yn, xn)
            part = plane.at[step, src, h]
            return remote(part, part, f_send.at[step, h], p_recv.at[step, src, h], dev(z, to, col))

        def arrived(q, h):
            part = plane.at[step, q, h]
            remote(part, part, f_send.at[step, h], p_recv.at[step, q, h], dev(z, xn, col)).wait_recv()

        def z_down(v, j):
            @pl.when(lowered(j))
            def _():
                z_copy(v, j).start()

        def up_copy(j):
            part = held.at[step, 0, :, pl.ds(j * ch, ch)]
            return remote(part, part, z_send.at[step, 0, j], z_recv.at[step, 0, j], dev((z + 1) % A, p, col))

        def each(action):
            def one(j, _):
                action(j)
                return 0

            lax.fori_loop(0, nj, one, 0)

        def end_chunk(j, action):
            @pl.when((z == A - 1) & lowered(j) & needed(z, j))
            def _():
                action(z_copy(z, j))

            if A > 1:
                @pl.when(z == 0)
                def _():
                    action(up_copy(j))

        @pl.when(z < A - 1)
        def _():
            each_chunk(z, z_down)

        end_chunk(0, lambda c: c.start())

        for h in range(lr):
            to_x(h).start()
            to_y(h).start()

        def cols_of(j):
            return pl.ds(pl.multiple_of(j * kw, kw), kw)

        def build(v, j):
            def one(i, _):
                h, m = i // ch, j * ch + i % ch
                hi, lo = sigma(held[step, v, h, m], (v * B + p) * lr + h, m)
                r0 = pl.multiple_of(h * orb, orb)
                c0 = pl.multiple_of(m * wide, wide)
                sx[v, pl.ds(r0, orb), pl.ds(c0, wide)] = hi
                sx[v, pl.ds(pl.multiple_of(lr * orb + r0, orb), orb), pl.ds(c0, wide)] = lo
                return 0

            lax.fori_loop(0, lr * ch, one, 0, unroll=UNROLL)

        def t_dot(v, j, q=None):
            ks = cols_of(j)
            us = pl.ds(0, pu * wide) if q is None else pl.ds(pl.multiple_of(q * lr * wide, lr * wide), lr * wide)
            both = dot(sx[v, :, ks], hat_hi[us, ks], NT)
            low = dot(sx[v, pl.ds(0, lr * orb), ks], hat_lo[us, ks], NT)
            acc_t[v, :, us] += both[: lr * orb] + (both[lr * orb :] + low)

        def t_rows(v, *qs):
            def one(v, j):
                for q in qs:
                    t_dot(v, j, q)

            each_chunk(v, one)

        def u_dot(v, j):
            @pl.when(reached(j))
            def _():
                def one(i, _):
                    h, m = i // ch, j * ch + i % ch
                    g = held[step, v, h, m]
                    r0 = pl.multiple_of(h * 2 * orb, 2 * orb)
                    r1 = pl.multiple_of(r0 + orb, orb)
                    c0 = pl.multiple_of((i % ch) * wide, wide)
                    hi, lo = split(g)
                    hx_hi[pl.ds(r0, orb), pl.ds(c0, wide)] = hi
                    hx_lo[pl.ds(r0, orb), pl.ds(c0, wide)] = lo
                    hi, lo = split(rot(g))
                    hx_hi[pl.ds(r1, orb), pl.ds(c0, wide)] = hi
                    hx_lo[pl.ds(r1, orb), pl.ds(c0, wide)] = lo
                    return 0

                lax.fori_loop(0, lr * ch, one, 0, unroll=UNROLL)
                ks = cols_of(j)
                hi, lo = sig_hi[:, ks], sig_lo[:, ks]
                ghi, glo = hx_hi[...], hx_lo[...]
                acc_u[v] += dot(hi, ghi, NT) + (dot(hi, glo, NT) + dot(lo, ghi, NT))

        def t_red(v, to):
            return remote(acc_t.at[v], red_t.at[step, v], rt_send.at[v], rt_recv.at[step, v], dev(z, p, to))

        def u_red(v, to):
            return remote(acc_u.at[v], red_u.at[step, v], ru_send.at[v], ru_recv.at[step, v], dev(z, p, to))

        def t_res(v):
            return remote(acc_t.at[v], res.at[step, z], t_send.at[v], t_recv.at[step, z], dev(v, p, col))

        def u_part(v, q, at):
            return (
                acc_u.at[v, pl.ds(pl.multiple_of(q * lr * orb, lr * orb), lr * orb), :],
                res.at[step, v, :, pl.ds(pl.multiple_of(at * lr * wide, lr * wide), lr * wide)],
            )

        def u_res(v, q):
            src, dst = u_part(v, q, p)
            return remote(src, dst, u_send.at[v, q], u_recv.at[step, v, p], dev(z, q, col))

        def place(owner):
            return (col + C - owner) % C

        down = (col + C - 1) % C

        def t_finish(v):
            k = place(cz)
            if C > 1:
                @pl.when(k > 0)
                def _():
                    if C > 2:
                        @pl.when(k < C - 1)
                        def _():
                            t_red(v, down).wait_recv()
                            acc_t[v] += red_t[step, v]

                    t_red(v, down).start()

            @pl.when(k == 0)
            def _():
                if C > 1:
                    t_red(v, down).wait_recv()

                @pl.when(v > z)
                def _():
                    if C > 1:
                        acc_t[v] += red_t[step, v]
                    t_res(v).start()

                @pl.when(v == z)
                def _():
                    if C > 1:
                        res[step, z] = acc_t[z] + red_t[step, z]
                    else:
                        res[step, z] = acc_t[z]

        def u_finish(v):
            k = place(v // ppc)
            if C > 1:
                @pl.when(k < C - 1)
                def _():
                    u_red(v, down).wait_recv()
                    acc_u[v] += red_u[step, v]

                @pl.when(k > 0)
                def _():
                    u_red(v, down).start()

            @pl.when(k == 0)
            def _():
                for q in (xn, yn, dn):
                    u_res(v, q).start()
                src, dst = u_part(v, p, p)
                dst[...] = src[...]

        def take(v, j):
            z_copy(v, j).wait_recv()
            z_down(v, j)

        def take_up(j):
            up_copy(j).wait_recv()

            @pl.when(z + 1 < A)
            def _():
                up_copy(j).start()

        above = (z > 0) & (z + 1 < A)

        def pass_on(j):
            end_chunk(j, lambda c: c.wait_send())
            if j + 1 < nj:
                end_chunk(j + 1, lambda c: c.start())

            @pl.when(above)
            def _():
                take_up(j)

                @pl.when(needed(z + 1, j))
                def _():
                    take(z + 1, j)

        def clear(v, _):
            acc_t[v] = jnp.zeros(acc_t.shape[1:], jnp.float32)
            acc_u[v] = jnp.zeros(acc_u.shape[1:], jnp.float32)
            return 0

        def prepare():
            sigma_plane(own, p)
            lax.fori_loop(z, A, clear, 0)
            acc_u[0] = jnp.zeros(acc_u.shape[1:], jnp.float32)

        def one_body():
            each_chunk(z, build)
            for h in range(lr):
                r0 = pl.multiple_of((p * lr + h) * 2 * orb, 2 * orb)
                g_hi = hat_hi[pl.ds(r0, 2 * orb), :]
                g_lo = hat_lo[pl.ds(r0, 2 * orb), :]
                h_acc[pl.ds(h * orb, orb), :] = dot(ham_hi, g_hi, NN) + (dot(ham_hi, g_lo, NN) + dot(ham_lo, g_hi, NN))
            t_rows(z, p)

        def neighbours():
            for h in range(lr):
                arrived(xn if h % 2 == 0 else yn, h)
                onward(h).start()

        hats(own, hat_hi, hat_lo, p * lr)
        work = [prepare, one_body, neighbours]
        for j in range(max(nj, len(work))):
            if j < nj:
                pass_on(j)
            if j < len(work):
                work[j]()

        @pl.when(above)
        def _():
            each_chunk(z + 1, build)
            t_rows(z + 1, p)

        for h in range(lr):
            arrived(yn if h % 2 == 0 else xn, h)
        for q in (xn, yn):
            hats(plane.at[step, q], hat_hi, hat_lo, q * lr)
            sigma_plane(plane.at[step, q], q)
        t_rows(z, xn, yn)

        @pl.when(above)
        def _():
            t_rows(z + 1, xn, yn)

        early = nj // 2

        @pl.when((z > 0) & (z + 2 < A))
        def _():
            def one(v, j):
                @pl.when(j < early)
                def _():
                    take(v, j)
                    build(v, j)
                    for q in (p, xn, yn):
                        t_dot(v, j, q)

            each_chunk(z + 2, one)

        for h in range(lr):
            arrived(dn, h)
        hats(plane.at[step, dn], hat_hi, hat_lo, dn * lr)
        sigma_plane(plane.at[step, dn], dn)

        t_rows(z, dn)
        t_finish(z)

        @pl.when(above)
        def _():
            t_rows(z + 1, dn)
            t_finish(z + 1)
            each_chunk(z + 1, u_dot)
            u_finish(z + 1)

        def late(v, _):
            def one(v, j):
                done = (v == z + 2) & (j < early)

                @pl.when(done)
                def _():
                    t_dot(v, j, dn)

                @pl.when(jnp.logical_not(done))
                def _():
                    take(v, j)
                    build(v, j)
                    t_dot(v, j)

                u_dot(v, j)

            each_chunk(v, one)
            t_finish(v)
            u_finish(v)
            return 0

        @pl.when(z > 0)
        def _():
            lax.fori_loop(z + 2, A, late, 0)
            @pl.when(z + 1 == A)
            def _():
                each(take_up)

            each(lambda j: u_dot(0, j))
            u_finish(0)

        @pl.when(z == 0)
        def _():
            def lowest(v, _):
                def one(j):
                    @pl.when(reached(j))
                    def _():
                        take(v, j)
                        u_dot(v, j)

                each(one)
                u_finish(v)
                return 0

            lax.fori_loop(1, A, lowest, 0)

        def collect(i, _):
            w = col * ppc + i

            in_plane = (w > z) | ((w == 0) & (z > 0))

            @pl.when((w < z) & (w > 0))
            def _():
                part = res.at[step, w]
                remote(part, part, t_send.at[w], t_recv.at[step, w], dev(z, xn, col)).wait_recv()

            @pl.when(in_plane)
            def _():
                for q in (xn, yn, dn):
                    part = res.at[step, w, :, pl.ds(pl.multiple_of(q * lr * wide, lr * wide), lr * wide)]
                    remote(part, part, u_send.at[w, q], u_recv.at[step, w, q], dev(z, xn, col)).wait_recv()

            def update(i, _):
                h, m = i // pu, i % pu
                u = (w - col * ppc) * pu + m
                r0 = pl.multiple_of(h * orb, orb)
                driven = h_acc[pl.ds(r0, orb), pl.ds(pl.multiple_of(u * wide, wide), wide)]
                driven = driven + res[step, w, pl.ds(r0, orb), pl.ds(pl.multiple_of(m * wide, wide), wide)]
                new = held[step, z, h, u] - time_step * rot(driven)

                @pl.when(step < STEPS - 1)
                def _():
                    held[step + 1, z, h, u] = new

                @pl.when(step == STEPS - 1)
                def _():
                    out[h, u] = new
                return 0

            lax.fori_loop(0, lr * pu, update, 0, unroll=UNROLL)
            return 0

        lax.fori_loop(0, ppc, collect, 0)

        for h in range(lr):
            to_x(h).wait_send()
            to_y(h).wait_send()
            onward(h).wait_send()

        def u_sent(v):
            ku = place(v // ppc)

            @pl.when(ku > 0)
            def _():
                u_red(v, down).wait_send()

            @pl.when(ku == 0)
            def _():
                for q in (xn, yn, dn):
                    u_res(v, q).wait_send()

        def left(v, j):
            @pl.when(lowered(j))
            def _():
                z_copy(v, j).wait_send()

        def sent(v, _):
            @pl.when((v > z) | (z < A - 1))
            def _():
                each_chunk(v, left)

            @pl.when((v == z) | (z > 0))
            def _():
                k = place(cz)

                @pl.when(k > 0)
                def _():
                    t_red(v, down).wait_send()

                @pl.when((k == 0) & (v > z))
                def _():
                    t_res(v).wait_send()

            @pl.when(v > z)
            def _():
                u_sent(v)
            return 0

        @pl.when(z > 0)
        def _():
            u_sent(0)

        if A > 1:
            @pl.when(above)
            def _():
                each(lambda j: up_copy(j).wait_send())

        lax.fori_loop(z, A, sent, 0)
        return 0

    lax.fori_loop(0, STEPS, step_body, 0)


def solution(mesh):
    rows, cols = mesh.shape["row"], mesh.shape["col"]
    planes = rows // GROUP

    def step(green, ham):
        lr, lc, orb, wide = green.shape
        pu = GROUP * lr
        nj = lc // min(CHUNK, lc)
        f32, bf16 = jnp.float32, jnp.bfloat16
        dma = pltpu.SemaphoreType.DMA
        big = (lr * orb, pu * wide)
        tall = (pu * orb, lr * wide)
        return pl.pallas_call(
            functools.partial(kernel, planes, cols),
            out_shape=jax.ShapeDtypeStruct(green.shape, f32),
            in_specs=[pl.BlockSpec(memory_space=pltpu.VMEM)] * 2,
            out_specs=pl.BlockSpec(memory_space=pltpu.VMEM),
            scratch_shapes=[
                pltpu.VMEM((STEPS, planes) + green.shape, f32),
                pltpu.VMEM((STEPS, GROUP) + green.shape, f32),
                pltpu.VMEM((STEPS, planes) + big, f32),
                pltpu.VMEM((STEPS, planes) + big, f32),
                pltpu.VMEM((STEPS, planes) + tall, f32),
                pltpu.VMEM((planes,) + big, f32),
                pltpu.VMEM((planes,) + tall, f32),
                pltpu.VMEM((pu * wide, lc * wide), bf16),
                pltpu.VMEM((pu * wide, lc * wide), bf16),
                pltpu.VMEM((pu * orb, lc * wide), bf16),
                pltpu.VMEM((pu * orb, lc * wide), bf16),
                pltpu.VMEM((planes, 2 * lr * orb, lc * wide), bf16),
                pltpu.VMEM((lr * wide, min(CHUNK, lc) * wide), bf16),
                pltpu.VMEM((lr * wide, min(CHUNK, lc) * wide), bf16),
                pltpu.VMEM((lr * orb, lc * wide), f32),
                dma((STEPS, planes, nj)), dma((STEPS, planes, nj)),
                dma((STEPS, lr)), dma((STEPS, lr)), dma((STEPS, lr)),
                dma((STEPS, GROUP, lr)),
                dma((planes,)), dma((STEPS, planes)),
                dma((planes,)), dma((STEPS, planes)),
                dma((planes,)), dma((STEPS, planes)),
                dma((planes, GROUP)), dma((STEPS, planes, GROUP)),
            ],
            compiler_params=pltpu.CompilerParams(
                collective_id=0, has_side_effects=True, vmem_limit_bytes=62 * 1024 * 1024
            ),
        )(green, ham)

    spec = P("row", "col", None, None)
    return jax.shard_map(step, mesh=mesh, in_specs=(spec, P()), out_specs=spec, check_vma=False)
```

```python
import functools

import jax
import jax.numpy as jnp
from jax import lax
from jax.experimental import pallas as pl
from jax.experimental.pallas import tpu as pltpu
from jax.sharding import PartitionSpec as P

STEPS = 2
time_step = 0.1

GROUP = 4
UNROLL = 8
CHUNK = 4
MESH = pl.DeviceIdType.MESH
NT = (((1,), (1,)), ((), ()))
NN = (((1,), (0,)), ((), ()))


def dot(a, b, dims):
    return lax.dot_general(a, b, dims, preferred_element_type=jnp.float32)


def split(x):
    hi = x.astype(jnp.bfloat16)
    lo = (x - hi.astype(jnp.float32)).astype(jnp.bfloat16)
    return hi, lo


def kernel(
    planes, cols, green, ham, out, held, plane, res, red_t, red_u,
    acc_t, acc_u, hat_hi, hat_lo, sig_hi, sig_lo, sx, hx_hi, hx_lo, h_acc,
    z_send, z_recv, x_send, y_send, f_send, p_recv,
    rt_send, rt_recv, ru_send, ru_recv, t_send, t_recv, u_send, u_recv,
):
    lr, lc, orb, wide = green.shape
    half = wide // 2
    B, A, C = GROUP, planes, cols
    pu = B * lr
    ppc = lc // pu
    ch = min(CHUNK, lc)
    nj = lc // ch
    kw = ch * wide

    row = lax.axis_index("row")
    col = lax.axis_index("col")
    z, p = row // B, row % B
    xn = p + 1 - 2 * (p % 2)
    yn = (p + 2) % B
    dn = (xn + 2) % B
    s_first = col * lc
    cz = z // ppc

    def dev(zz, pp, cc):
        return (zz * B + pp, cc)

    def remote(src, dst, ss, rs, to):
        return pltpu.make_async_remote_copy(
            src_ref=src, dst_ref=dst, send_sem=ss, recv_sem=rs, device_id=to, device_id_type=MESH
        )

    bar = pltpu.get_barrier_semaphore()
    for q in (xn, yn, dn):
        pl.semaphore_signal(bar, inc=1, device_id=dev(z, q, col), device_id_type=MESH)
    for k in range(1, A):
        pl.semaphore_signal(bar, inc=1, device_id=dev((z + k) % A, p, col), device_id_type=MESH)
    for k in range(1, C):
        pl.semaphore_signal(bar, inc=1, device_id=dev(z, p, (col + k) % C), device_id_type=MESH)

    lane = lax.broadcasted_iota(jnp.int32, (orb, wide), 1)
    sign = jnp.where(lane < half, jnp.float32(-1.0), jnp.float32(1.0))

    def rot(x):
        return pltpu.roll(x, half, 1) * sign

    def copy_in(i, _):
        h, m = i // lc, i % lc
        held[0, z, h, m] = green[h, m]
        return 0

    lax.fori_loop(0, lr * lc, copy_in, 0, unroll=UNROLL)
    pl.semaphore_wait(bar, (B - 1) + (A - 1) + (C - 1))

    ham_hi, ham_lo = split(ham[...])

    def needed(v, j):
        return s_first + j * ch <= (v * B + p) * lr + lr - 1

    def reached(j):
        return s_first + j * ch <= z * pu + pu - 1

    def lowered(j):
        return (z > 1) | ((z == 1) & (s_first + j * ch <= pu - 1))

    def hats(src, hi_ref, lo_ref, first):
        def one(i, _):
            h, m = i // lc, i % lc
            g = src[h, m]
            r0 = pl.multiple_of((first + h) * 2 * orb, 2 * orb)
            c0 = pl.multiple_of(m * wide, wide)
            hi, lo = split(g)
            hi_ref[pl.ds(r0, orb), pl.ds(c0, wide)] = hi
            lo_ref[pl.ds(r0, orb), pl.ds(c0, wide)] = lo
            hi, lo = split(rot(g))
            r1 = pl.multiple_of(r0 + orb, orb)
            hi_ref[pl.ds(r1, orb), pl.ds(c0, wide)] = hi
            lo_ref[pl.ds(r1, orb), pl.ds(c0, wide)] = lo
            return 0

        lax.fori_loop(0, lr * lc, one, 0, unroll=UNROLL)

    def sigma(g, t, m):
        s = s_first + m
        weight = jnp.where(s < t, jnp.float32(time_step), jnp.where(s == t, jnp.float32(0.5 * time_step), jnp.float32(0.0)))
        sq = g * g
        return split(weight * ((sq + pltpu.roll(sq, half, 1)) * g))

    def sigma_plane(src, q):
        def chunk(j, _):
            @pl.when(reached(j))
            def _():
                def one(i, _):
                    h, m = i // ch, j * ch + i % ch
                    hi, lo = sigma(src[h, m], (z * B + q) * lr + h, m)
                    r0 = pl.multiple_of((q * lr + h) * orb, orb)
                    c0 = pl.multiple_of(m * wide, wide)
                    sig_hi[pl.ds(r0, orb), pl.ds(c0, wide)] = hi
                    sig_lo[pl.ds(r0, orb), pl.ds(c0, wide)] = lo
                    return 0

                lax.fori_loop(0, lr * ch, one, 0, unroll=UNROLL)
            return 0

        lax.fori_loop(0, nj, chunk, 0)

    def step_body(step, _):
        own = held.at[step, z]

        def z_copy(v, j):
            part = held.at[step, v, :, pl.ds(j * ch, ch)]
            return remote(part, part, z_send.at[step, v, j], z_recv.at[step, v, j], dev((z + A - 1) % A, p, col))

        def each_chunk(v, action):
            def one(j, _):
                @pl.when(needed(v, j))
                def _():
                    action(v, j)
                return 0

            lax.fori_loop(0, nj, one, 0)

        def to_x(h):
            return remote(own.at[h], plane.at[step, p, h], x_send.at[step, h], p_recv.at[step, p, h], dev(z, xn, col))

        def to_y(h):
            return remote(own.at[h], plane.at[step, p, h], y_send.at[step, h], p_recv.at[step, p, h], dev(z, yn, col))

        def onward(h):
            src, to = (xn, yn) if h % 2 == 0 else (yn, xn)
            part = plane.at[step, src, h]
            return remote(part, part, f_send.at[step, h], p_recv.at[step, src, h], dev(z, to, col))

        def arrived(q, h):
            part = plane.at[step, q, h]
            remote(part, part, f_send.at[step, h], p_recv.at[step, q, h], dev(z, xn, col)).wait_recv()

        def z_down(v, j):
            @pl.when(lowered(j))
            def _():
                z_copy(v, j).start()

        def up_copy(j):
            part = held.at[step, 0, :, pl.ds(j * ch, ch)]
            return remote(part, part, z_send.at[step, 0, j], z_recv.at[step, 0, j], dev((z + 1) % A, p, col))

        def each(action):
            def one(j, _):
                action(j)
                return 0

            lax.fori_loop(0, nj, one, 0)

        def end_chunk(j, action):
            @pl.when((z == A - 1) & lowered(j) & needed(z, j))
            def _():
                action(z_copy(z, j))

            if A > 1:
                @pl.when(z == 0)
                def _():
                    action(up_copy(j))

        @pl.when(z < A - 1)
        def _():
            each_chunk(z, z_down)

        end_chunk(0, lambda c: c.start())

        for h in range(lr):
            (to_x(h) if h % 2 == 0 else to_y(h)).start()

        def cols_of(j):
            return pl.ds(pl.multiple_of(j * kw, kw), kw)

        def build(v, j):
            def one(i, _):
                h, m = i // ch, j * ch + i % ch
                hi, lo = sigma(held[step, v, h, m], (v * B + p) * lr + h, m)
                r0 = pl.multiple_of(h * orb, orb)
                c0 = pl.multiple_of(m * wide, wide)
                sx[v, pl.ds(r0, orb), pl.ds(c0, wide)] = hi
                sx[v, pl.ds(pl.multiple_of(lr * orb + r0, orb), orb), pl.ds(c0, wide)] = lo
                return 0

            lax.fori_loop(0, lr * ch, one, 0, unroll=UNROLL)

        def t_dot(v, j, q=None):
            ks = cols_of(j)
            us = pl.ds(0, pu * wide) if q is None else pl.ds(pl.multiple_of(q * lr * wide, lr * wide), lr * wide)
            both = dot(sx[v, :, ks], hat_hi[us, ks], NT)
            low = dot(sx[v, pl.ds(0, lr * orb), ks], hat_lo[us, ks], NT)
            acc_t[v, :, us] += both[: lr * orb] + (both[lr * orb :] + low)

        def t_rows(v, *qs):
            def one(v, j):
                for q in qs:
                    t_dot(v, j, q)

            each_chunk(v, one)

        def u_dot(v, j):
            @pl.when(reached(j))
            def _():
                def one(i, _):
                    h, m = i // ch, j * ch + i % ch
                    g = held[step, v, h, m]
                    r0 = pl.multiple_of(h * 2 * orb, 2 * orb)
                    r1 = pl.multiple_of(r0 + orb, orb)
                    c0 = pl.multiple_of((i % ch) * wide, wide)
                    hi, lo = split(g)
                    hx_hi[pl.ds(r0, orb), pl.ds(c0, wide)] = hi
                    hx_lo[pl.ds(r0, orb), pl.ds(c0, wide)] = lo
                    hi, lo = split(rot(g))
                    hx_hi[pl.ds(r1, orb), pl.ds(c0, wide)] = hi
                    hx_lo[pl.ds(r1, orb), pl.ds(c0, wide)] = lo
                    return 0

                lax.fori_loop(0, lr * ch, one, 0, unroll=UNROLL)
                ks = cols_of(j)
                hi, lo = sig_hi[:, ks], sig_lo[:, ks]
                ghi, glo = hx_hi[...], hx_lo[...]
                acc_u[v] += dot(hi, ghi, NT) + (dot(hi, glo, NT) + dot(lo, ghi, NT))

        def t_red(v, to):
            return remote(acc_t.at[v], red_t.at[step, v], rt_send.at[v], rt_recv.at[step, v], dev(z, p, to))

        def u_red(v, to):
            return remote(acc_u.at[v], red_u.at[step, v], ru_send.at[v], ru_recv.at[step, v], dev(z, p, to))

        def t_res(v):
            return remote(acc_t.at[v], res.at[step, z], t_send.at[v], t_recv.at[step, z], dev(v, p, col))

        def u_part(v, q, at):
            return (
                acc_u.at[v, pl.ds(pl.multiple_of(q * lr * orb, lr * orb), lr * orb), :],
                res.at[step, v, :, pl.ds(pl.multiple_of(at * lr * wide, lr * wide), lr * wide)],
            )

        def u_res(v, q):
            src, dst = u_part(v, q, p)
            return remote(src, dst, u_send.at[v, q], u_recv.at[step, v, p], dev(z, q, col))

        def place(owner):
            return (col + C - owner) % C

        down = (col + C - 1) % C

        def t_finish(v):
            k = place(cz)
            if C > 1:
                @pl.when(k > 0)
                def _():
                    if C > 2:
                        @pl.when(k < C - 1)
                        def _():
                            t_red(v, down).wait_recv()
                            acc_t[v] += red_t[step, v]

                    t_red(v, down).start()

            @pl.when(k == 0)
            def _():
                if C > 1:
                    t_red(v, down).wait_recv()

                @pl.when(v > z)
                def _():
                    if C > 1:
                        acc_t[v] += red_t[step, v]
                    t_res(v).start()

                @pl.when(v == z)
                def _():
                    if C > 1:
                        res[step, z] = acc_t[z] + red_t[step, z]
                    else:
                        res[step, z] = acc_t[z]

        def u_finish(v):
            k = place(v // ppc)
            if C > 1:
                @pl.when(k < C - 1)
                def _():
                    u_red(v, down).wait_recv()
                    acc_u[v] += red_u[step, v]

                @pl.when(k > 0)
                def _():
                    u_red(v, down).start()

            @pl.when(k == 0)
            def _():
                for q in (xn, yn, dn):
                    u_res(v, q).start()
                src, dst = u_part(v, p, p)
                dst[...] = src[...]

        def take(v, j):
            z_copy(v, j).wait_recv()
            z_down(v, j)

        def take_up(j):
            up_copy(j).wait_recv()

            @pl.when(z + 1 < A)
            def _():
                up_copy(j).start()

        above = (z > 0) & (z + 1 < A)

        def pass_on(j):
            end_chunk(j, lambda c: c.wait_send())
            if j + 1 < nj:
                end_chunk(j + 1, lambda c: c.start())

            @pl.when(above)
            def _():
                take_up(j)

                @pl.when(needed(z + 1, j))
                def _():
                    take(z + 1, j)

        def clear(v, _):
            acc_t[v] = jnp.zeros(acc_t.shape[1:], jnp.float32)
            acc_u[v] = jnp.zeros(acc_u.shape[1:], jnp.float32)
            return 0

        def prepare():
            sigma_plane(own, p)
            lax.fori_loop(z, A, clear, 0)
            acc_u[0] = jnp.zeros(acc_u.shape[1:], jnp.float32)
            for h in range(lr):
                (to_y(h) if h % 2 == 0 else to_x(h)).start()

        def one_body():
            each_chunk(z, build)
            for h in range(lr):
                r0 = pl.multiple_of((p * lr + h) * 2 * orb, 2 * orb)
                g_hi = hat_hi[pl.ds(r0, 2 * orb), :]
                g_lo = hat_lo[pl.ds(r0, 2 * orb), :]
                h_acc[pl.ds(h * orb, orb), :] = dot(ham_hi, g_hi, NN) + (dot(ham_hi, g_lo, NN) + dot(ham_lo, g_hi, NN))
            t_rows(z, p)

        def neighbours():
            for h in range(lr):
                arrived(xn if h % 2 == 0 else yn, h)
                onward(h).start()

        hats(own, hat_hi, hat_lo, p * lr)
        work = [prepare, neighbours, one_body]
        for j in range(max(nj, len(work))):
            if j < nj:
                pass_on(j)
            if j < len(work):
                work[j]()

        @pl.when(above)
        def _():
            each_chunk(z + 1, build)
            t_rows(z + 1, p)

        for h in range(lr):
            arrived(yn if h % 2 == 0 else xn, h)
        for q in (xn, yn):
            hats(plane.at[step, q], hat_hi, hat_lo, q * lr)
            sigma_plane(plane.at[step, q], q)
        t_rows(z, xn, yn)

        @pl.when(above)
        def _():
            t_rows(z + 1, xn, yn)

        early = nj // 2

        @pl.when((z > 0) & (z + 2 < A))
        def _():
            def one(v, j):
                @pl.when(j < early)
                def _():
                    take(v, j)
                    build(v, j)
                    for q in (p, xn, yn):
                        t_dot(v, j, q)

            each_chunk(z + 2, one)

        for h in range(lr):
            arrived(dn, h)
        hats(plane.at[step, dn], hat_hi, hat_lo, dn * lr)
        sigma_plane(plane.at[step, dn], dn)

        t_rows(z, dn)
        t_finish(z)

        @pl.when(above)
        def _():
            t_rows(z + 1, dn)
            t_finish(z + 1)
            each_chunk(z + 1, u_dot)
            u_finish(z + 1)

        def late(v, _):
            def one(v, j):
                done = (v == z + 2) & (j < early)

                @pl.when(done)
                def _():
                    t_dot(v, j, dn)

                @pl.when(jnp.logical_not(done))
                def _():
                    take(v, j)
                    build(v, j)
                    t_dot(v, j)

                u_dot(v, j)

            each_chunk(v, one)
            t_finish(v)
            u_finish(v)
            return 0

        @pl.when(z > 0)
        def _():
            lax.fori_loop(z + 2, A, late, 0)
            @pl.when(z + 1 == A)
            def _():
                each(take_up)

            each(lambda j: u_dot(0, j))
            u_finish(0)

        @pl.when(z == 0)
        def _():
            def lowest(v, _):
                def one(j):
                    @pl.when(reached(j))
                    def _():
                        take(v, j)
                        u_dot(v, j)

                each(one)
                u_finish(v)
                return 0

            lax.fori_loop(1, A, lowest, 0)

        def collect(i, _):
            w = col * ppc + i

            in_plane = (w > z) | ((w == 0) & (z > 0))

            @pl.when((w < z) & (w > 0))
            def _():
                part = res.at[step, w]
                remote(part, part, t_send.at[w], t_recv.at[step, w], dev(z, xn, col)).wait_recv()

            @pl.when(in_plane)
            def _():
                for q in (xn, yn, dn):
                    part = res.at[step, w, :, pl.ds(pl.multiple_of(q * lr * wide, lr * wide), lr * wide)]
                    remote(part, part, u_send.at[w, q], u_recv.at[step, w, q], dev(z, xn, col)).wait_recv()

            def update(i, _):
                h, m = i // pu, i % pu
                u = (w - col * ppc) * pu + m
                r0 = pl.multiple_of(h * orb, orb)
                driven = h_acc[pl.ds(r0, orb), pl.ds(pl.multiple_of(u * wide, wide), wide)]
                driven = driven + res[step, w, pl.ds(r0, orb), pl.ds(pl.multiple_of(m * wide, wide), wide)]
                new = held[step, z, h, u] - time_step * rot(driven)

                @pl.when(step < STEPS - 1)
                def _():
                    held[step + 1, z, h, u] = new

                @pl.when(step == STEPS - 1)
                def _():
                    out[h, u] = new
                return 0

            lax.fori_loop(0, lr * pu, update, 0, unroll=UNROLL)
            return 0

        lax.fori_loop(0, ppc, collect, 0)

        for h in range(lr):
            to_x(h).wait_send()
            to_y(h).wait_send()
            onward(h).wait_send()

        def u_sent(v):
            ku = place(v // ppc)

            @pl.when(ku > 0)
            def _():
                u_red(v, down).wait_send()

            @pl.when(ku == 0)
            def _():
                for q in (xn, yn, dn):
                    u_res(v, q).wait_send()

        def left(v, j):
            @pl.when(lowered(j))
            def _():
                z_copy(v, j).wait_send()

        def sent(v, _):
            @pl.when((v > z) | (z < A - 1))
            def _():
                each_chunk(v, left)

            @pl.when((v == z) | (z > 0))
            def _():
                k = place(cz)

                @pl.when(k > 0)
                def _():
                    t_red(v, down).wait_send()

                @pl.when((k == 0) & (v > z))
                def _():
                    t_res(v).wait_send()

            @pl.when(v > z)
            def _():
                u_sent(v)
            return 0

        @pl.when(z > 0)
        def _():
            u_sent(0)

        if A > 1:
            @pl.when(above)
            def _():
                each(lambda j: up_copy(j).wait_send())

        lax.fori_loop(z, A, sent, 0)
        return 0

    lax.fori_loop(0, STEPS, step_body, 0)


def solution(mesh):
    rows, cols = mesh.shape["row"], mesh.shape["col"]
    planes = rows // GROUP

    def step(green, ham):
        lr, lc, orb, wide = green.shape
        pu = GROUP * lr
        nj = lc // min(CHUNK, lc)
        f32, bf16 = jnp.float32, jnp.bfloat16
        dma = pltpu.SemaphoreType.DMA
        big = (lr * orb, pu * wide)
        tall = (pu * orb, lr * wide)
        return pl.pallas_call(
            functools.partial(kernel, planes, cols),
            out_shape=jax.ShapeDtypeStruct(green.shape, f32),
            in_specs=[pl.BlockSpec(memory_space=pltpu.VMEM)] * 2,
            out_specs=pl.BlockSpec(memory_space=pltpu.VMEM),
            scratch_shapes=[
                pltpu.VMEM((STEPS, planes) + green.shape, f32),
                pltpu.VMEM((STEPS, GROUP) + green.shape, f32),
                pltpu.VMEM((STEPS, planes) + big, f32),
                pltpu.VMEM((STEPS, planes) + big, f32),
                pltpu.VMEM((STEPS, planes) + tall, f32),
                pltpu.VMEM((planes,) + big, f32),
                pltpu.VMEM((planes,) + tall, f32),
                pltpu.VMEM((pu * wide, lc * wide), bf16),
                pltpu.VMEM((pu * wide, lc * wide), bf16),
                pltpu.VMEM((pu * orb, lc * wide), bf16),
                pltpu.VMEM((pu * orb, lc * wide), bf16),
                pltpu.VMEM((planes, 2 * lr * orb, lc * wide), bf16),
                pltpu.VMEM((lr * wide, min(CHUNK, lc) * wide), bf16),
                pltpu.VMEM((lr * wide, min(CHUNK, lc) * wide), bf16),
                pltpu.VMEM((lr * orb, lc * wide), f32),
                dma((STEPS, planes, nj)), dma((STEPS, planes, nj)),
                dma((STEPS, lr)), dma((STEPS, lr)), dma((STEPS, lr)),
                dma((STEPS, GROUP, lr)),
                dma((planes,)), dma((STEPS, planes)),
                dma((planes,)), dma((STEPS, planes)),
                dma((planes,)), dma((STEPS, planes)),
                dma((planes, GROUP)), dma((STEPS, planes, GROUP)),
            ],
            compiler_params=pltpu.CompilerParams(
                collective_id=0, has_side_effects=True, vmem_limit_bytes=62 * 1024 * 1024
            ),
        )(green, ham)

    spec = P("row", "col", None, None)
    return jax.shard_map(step, mesh=mesh, in_specs=(spec, P()), out_specs=spec, check_vma=False)
```
